128 devices in a mesh: blk: 8 (over y, x_hi), dp: 16 (over x_lo, z, core).
Axes of the slice: x: 4 (x_hi: 2, x_lo: 2; x = x_hi * 2 + x_lo), y: 4, z: 4, core: 2. Of those that a mesh axis runs over, the one named last changes fastest.
Arguments:
- proj: float32 [16384, 128], P(('blk', 'dp')), may hold values from -4 to 4
- partner: int32 [16384], replicated, may hold values from 0 to 16383, as said below
Outputs:
- loss: float32 [], replicated
- grad: float32 [16384, 128], P(('blk', 'dp'))
The draws below stay inside these ranges and needn't reach their ends.
Inputs may be any that keep to these rules, and one draw needn't show every extreme that they name: partner is an involution without fixed points: partner[partner[i]] = i and partner[i] != i.
All inputs are finite; a program needn't handle non-finite values.
Results may differ from the reference program's by a relative error of at most 0.0042.
Values may be sent and summed in bfloat16 or wider, within the bound.
No kernel may reach another device: no remote copies, remote signals or barrier semaphores. Data moves between devices by JAX's collectives and lax.ppermute only.
A program may use at most 64 MiB of HBM per device.

```python
import math
import jax
import jax.numpy as jnp
from jax import lax

PROJ = 128
VIEWS = 16384


def shared_pairs(key, total):
    order = jax.random.permutation(key, total)
    slot = jnp.arange(total)
    mate = order[slot + 1 - 2 * (slot % 2)]
    partner = jnp.zeros((total,), jnp.int32).at[order].set(mate.astype(jnp.int32))
    couple = jnp.zeros((total,), jnp.int32).at[order].set((slot // 2).astype(jnp.int32))
    return (partner, couple)


def draw_partner(key, part):
    partner, couple = shared_pairs(key, VIEWS)
    return partner


def draw_proj(key, part):
    partner, couple = shared_pairs(key, VIEWS)
    key = jax.random.fold_in(key, 7)
    keys = jax.random.split(key, 8)
    classes = max(VIEWS // 64, 2)
    first = jax.random.randint(keys[5], (VIEWS // 2,), 0, classes)
    second = jax.random.randint(keys[6], (VIEWS // 2,), 0, classes)
    kind = first * second // classes
    strength = jax.random.uniform(keys[7], (classes,), jnp.float32, 0.6, 1.0)
    direction = jax.random.truncated_normal(keys[4], -4.0, 4.0, (classes, PROJ), jnp.float32)
    base = jax.random.truncated_normal(keys[0], -4.0, 4.0, (VIEWS // 2, PROJ), jnp.float32)
    noise = jax.random.truncated_normal(keys[1], -4.0, 4.0, (VIEWS, PROJ), jnp.float32)
    coupled = strength[kind][:, None] * direction[kind] + 0.6 * base
    spread = 0.3 + 1.2 * jnp.arange(VIEWS, dtype=jnp.float32) / VIEWS
    row_scale = jnp.exp(jax.random.uniform(keys[2], (VIEWS, 1), jnp.float32, jnp.log(0.5), jnp.log(5.0)))
    values = row_scale * (coupled[couple] + spread[:, None] * noise) / 16.0
    return values.astype(jnp.float32)


def setup_inputs(seed: int = 0) -> dict:
    splits = jax.random.split(jax.random.key(seed), 3)
    proj = draw_proj(jax.random.fold_in(splits[2], 71), 0)
    partner = draw_partner(jax.random.fold_in(splits[2], 71), 0)
    return dict(proj=proj, partner=partner)


INV_TEMP = 10.0
EPS = 1e-06

def reference(proj, partner):
    views = proj.shape[0]
    radius = jnp.sqrt(lax.optimization_barrier(jnp.sum(proj * proj, axis=1, keepdims=True)) + EPS)
    unit = proj / radius
    unit_w = unit.astype(jnp.bfloat16).astype(jnp.float32)
    ids = jnp.arange(views, dtype=jnp.int32)
    size = math.gcd(views, 512)
    starts = (jnp.arange(views // size) * size).astype(jnp.int32)

    def scores_of(start):
        rows = lax.dynamic_slice_in_dim(unit_w, start, size, 0)
        mates = lax.dynamic_slice_in_dim(partner, start, size, 0)
        row_ids = start + jnp.arange(size, dtype=jnp.int32)
        scores = jnp.dot(rows, unit_w.T, precision=lax.Precision.HIGHEST) * INV_TEMP
        expo = jnp.where(row_ids[:, None] == ids[None, :], 0.0, jnp.exp(scores - INV_TEMP))
        marks = mates[:, None] == ids[None, :]
        return (scores, expo, marks)

    def first_pass(start):
        scores, expo, marks = scores_of(start)
        return (lax.optimization_barrier(jnp.sum(expo, axis=1)), lax.optimization_barrier(jnp.sum(jnp.where(marks, scores, 0.0), axis=1)))
    esum, pos = lax.map(first_pass, starts)
    esum = esum.reshape(views)
    pos = pos.reshape(views)
    loss = jnp.mean(INV_TEMP + jnp.log(esum) - pos)

    def second_pass(start):
        scores, expo, marks = scores_of(start)
        own_e = lax.dynamic_slice_in_dim(esum, start, size, 0)
        weight = (expo / own_e[:, None] + expo / esum[None, :] - 2.0 * marks.astype(jnp.float32)).astype(jnp.bfloat16)
        return jnp.dot(weight.astype(jnp.float32), unit_w, precision=lax.Precision.HIGHEST)
    accum = lax.map(second_pass, starts).reshape(views, proj.shape[1])
    dunit = accum * INV_TEMP
    grad = (dunit - unit * lax.optimization_barrier(jnp.sum(unit * dunit, axis=1, keepdims=True))) / radius
    return (loss, grad)
```

```python
import functools
import math

import jax
import jax.numpy as jnp
from jax import lax
from jax.experimental import pallas as pl
from jax.experimental.pallas import tpu as pltpu
from jax.sharding import Mesh, PartitionSpec as P

EPS = 1e-06
INV_TEMP = 10.0
SCALE = INV_TEMP * math.log2(math.e)

ROWS = 128
NXY = 16
NZ = 4
NCO = 2
NDEV = NXY * NZ * NCO
VIEWS = NDEV * ROWS
XY = ("y", "xh", "xl")
ALL = ("y", "xh", "xl", "z", "co")
CHUNK = 256
F32 = jnp.float32
BF16 = jnp.bfloat16
VMEM = pl.BlockSpec(memory_space=pltpu.VMEM)
SMEM = pl.BlockSpec(memory_space=pltpu.SMEM)


def call(body, outs, scratch=(), flops=0, nbytes=0, exps=0):
    def run(*args):
        return pl.pallas_call(
            body,
            out_shape=outs,
            in_specs=[SMEM if a.dtype == jnp.int32 and a.ndim == 1 else VMEM for a in args],
            out_specs=[VMEM] * len(outs),
            scratch_shapes=list(scratch),
            compiler_params=pltpu.CompilerParams(vmem_limit_bytes=24 * 2**20),
            cost_estimate=pl.CostEstimate(flops=flops, bytes_accessed=nbytes, transcendentals=exps),
        )(*args)

    return run


def sds(shape, dtype=F32):
    return jax.ShapeDtypeStruct(shape, dtype)


def dot_nt(a, b):
    return lax.dot_general(a, b, (((1,), (1,)), ((), ())), preferred_element_type=F32)


def dot_nn(a, b):
    return lax.dot_general(a, b, (((1,), (0,)), ((), ())), preferred_element_type=F32)


def down_rows(row):
    return jnp.transpose(jnp.broadcast_to(row, (ROWS, ROWS)))


def norm_kernel(x_ref, u_ref, copies_ref):
    x = x_ref[...]
    radius = jnp.sqrt(jnp.sum(x * x, axis=1, keepdims=True) + EPS)
    unit = (x / radius).astype(BF16)
    u_ref[...] = unit
    copies_ref[...] = jnp.broadcast_to(unit[None], (NXY, ROWS, ROWS))


def expo(s):
    return jnp.exp2(s * SCALE)


def clear_self(e, col0, own_col):
    col = lax.broadcasted_iota(jnp.int32, e.shape, 1) + (col0 - own_col)
    row = lax.broadcasted_iota(jnp.int32, e.shape, 0)
    return jnp.where(col == row, 0.0, e)


def sums_kernel(own_half, *refs):
    n_in = 7 if own_half else 10
    place_ref, u0, u1, u2, u3, c_ref, mate_ref = refs[:7]
    outs = refs[n_in:-3]
    e_ref, m_ref, sum_ref = refs[-3:]
    z, co, xy = place_ref[0], place_ref[1], place_ref[2]
    cols = c_ref.shape[0]
    half = co if own_half else 1 - co
    mates = mate_ref[...]
    here = (((mates >> 8) & 3) == z) & (((mates >> 7) & 1) == half)
    local = jnp.where(here, ((mates >> 10) << 7) | (mates & 127), -1)
    lane = lax.broadcasted_iota(jnp.int32, (ROWS, CHUNK), 1)
    for r, u_ref in enumerate((u0, u1, u2, u3)):
        rows = slice(r * ROWS, (r + 1) * ROWS)
        u = u_ref[...]
        mate = down_rows(local[r : r + 1])
        mate = jnp.concatenate([mate] * (CHUNK // ROWS), axis=1)
        total = jnp.zeros((ROWS, ROWS), F32)
        for c in range(0, cols, CHUNK):
            e = expo(dot_nt(u, c_ref[c : c + CHUNK]))
            if own_half and r == 0:
                e = clear_self(e, c, xy * ROWS)
            for k in range(0, CHUNK, ROWS):
                total = total + e[:, k : k + ROWS]
            e_ref[rows, c : c + CHUNK] = e.astype(BF16)
            m_ref[rows, c : c + CHUNK] = jnp.where(mate == lane + c, 1.0, 0.0).astype(BF16)
        sum_ref[r : r + 1, :] = jnp.sum(jnp.transpose(total), axis=0, keepdims=True)
    a = dot_nn(e_ref[...], c_ref[...])
    p = dot_nn(m_ref[...], c_ref[...])
    if own_half:
        outs[0][...] = sum_ref[...]
        outs[1][...] = a
        outs[2][...] = p
        return
    sum_in, a_in, p_in = refs[7:10]
    a = a + a_in[...]
    p = p + p_in[...]
    pos = jnp.zeros((ROWS, ROWS), F32)
    for r, u_ref in enumerate((u0, u1, u2, u3)):
        rows = slice(r * ROWS, (r + 1) * ROWS)
        outs[1 + r][0:ROWS] = a[rows]
        outs[1 + r][ROWS : 2 * ROWS] = p[rows]
        pos = pos + u_ref[...].astype(F32) * p[rows]
    sums = sum_ref[...] + sum_in[...]
    pos = INV_TEMP * jnp.sum(pos, axis=0, keepdims=True)
    for k in range(NZ):
        r = lax.rem(k - z + NZ, NZ)
        row = jnp.zeros((1, ROWS), F32)
        for q in range(NZ):
            row = jnp.where(r == q, sums[q : q + 1], row)
        piece = jnp.concatenate([row, pos], axis=1)
        for xy_to in range(NXY):
            for co_to in range(NCO):
                outs[0][xy_to * 8 + k * 2 + co_to] = piece


def grads_kernel(place_ref, u0, u1, u2, u3, own_ref, other_ref, got_ref, b0, b1, b2, b3, aux_ref, inv_ref, w_ref):
    co, xy = place_ref[1], place_ref[2]
    logs = jnp.zeros((1, ROWS), F32)
    for k in range(NXY):
        for c in range(NCO):
            total = got_ref[k * 8 + c, :, 0:ROWS]
            for z in range(1, NZ):
                total = total + got_ref[k * 8 + z * 2 + c, :, 0:ROWS]
            logs = logs + jnp.log(total)
            inv_ref[c, :, k * ROWS : (k + 1) * ROWS] = 1.0 / total
    pos = got_ref[0, :, ROWS:]
    for k in range(1, NDEV):
        pos = pos + got_ref[k, :, ROWS:]
    own_col = pl.multiple_of(xy * ROWS, ROWS)
    aux_ref[0:1] = inv_ref[co, :, pl.ds(own_col, ROWS)]
    aux_ref[1:2] = pos
    aux_ref[2:8] = jnp.zeros((6, ROWS), F32)
    for r, (u_ref, b_ref) in enumerate(zip((u0, u1, u2, u3), (b0, b1, b2, b3))):
        rows = slice(r * ROWS, (r + 1) * ROWS)
        u = u_ref[...]
        for h, c_ref in enumerate((own_ref, other_ref)):
            cols = c_ref.shape[0]
            for c in range(0, cols, CHUNK):
                e = expo(dot_nt(u, c_ref[c : c + CHUNK]))
                if h == 0 and r == 0:
                    e = clear_self(e, c, xy * ROWS)
                half = co if h == 0 else 1 - co
                w_ref[h, rows, c : c + CHUNK] = (e * inv_ref[half, :, c : c + CHUNK]).astype(BF16)
    b = dot_nn(w_ref[0], own_ref[...]) + dot_nn(w_ref[1], other_ref[...])
    for r, b_ref in enumerate((b0, b1, b2, b3)):
        b_ref[0:ROWS] = b[r * ROWS : (r + 1) * ROWS]
        b_ref[ROWS : ROWS + 1] = logs
        b_ref[ROWS + 1 :] = jnp.zeros((7, ROWS), F32)


def final_kernel(place_ref, x_ref, aux_ref, a0, a1, a2, a3, b0, b1, b2, b3, loss_ref, grad_ref, log_ref):
    z = place_ref[0]
    x = x_ref[...]
    radius = jnp.sqrt(jnp.sum(x * x, axis=1, keepdims=True) + EPS)
    unit = x / radius
    ap = a0[...] + a1[...] + a2[...] + a3[...]
    b = b0[0:ROWS] + b1[0:ROWS] + b2[0:ROWS] + b3[0:ROWS]
    inv = down_rows(aux_ref[0:1])
    d = INV_TEMP * (ap[0:ROWS] * inv + b - 2.0 * ap[ROWS:])
    grad_ref[...] = (d - unit * jnp.sum(unit * d, axis=1, keepdims=True)) / radius
    for r, b_ref in enumerate((b0, b1, b2, b3)):
        log_ref[lax.rem(z - r + NZ, NZ)] = b_ref[ROWS : ROWS + 8]
    logs = log_ref[0, 0:1]
    for k in range(1, NZ):
        logs = logs + log_ref[k, 0:1]
    loss_ref[...] = jnp.sum(logs - aux_ref[1:2], axis=1, keepdims=True) / VIEWS


def shift(x, by):
    return lax.ppermute(x, "z", [((k + by) % NZ, k) for k in range(NZ)])


def body(proj, partner):
    y, xh, xl = (lax.axis_index(a) for a in XY)
    z, co = lax.axis_index("z"), lax.axis_index("co")
    xy = (y * 2 + xh) * 2 + xl
    place = jnp.stack([z, co, xy]).astype(jnp.int32)
    unit, copies = call(norm_kernel, [sds((ROWS, ROWS), BF16), sds((NXY, ROWS, ROWS), BF16)])(proj)
    plane = lax.all_to_all(copies, XY, 0, 0, tiled=True)
    rows = [unit] + [shift(unit, r) for r in range(1, NZ)]
    mates = partner.reshape(NXY, NZ, NCO, ROWS)
    mates = lax.dynamic_slice(mates, (xy, 0, co, 0), (1, NZ, 1, ROWS)).reshape(NZ, ROWS)
    mates = jnp.concatenate([mates, mates])
    mates = lax.dynamic_slice_in_dim(mates, z, NZ, 0)
    plane, mates, *rows = lax.optimization_barrier((plane, mates, *rows))
    other = lax.ppermute(plane, "co", [(0, 1), (1, 0)])
    cols = NXY * ROWS
    plane = plane.reshape(cols, ROWS)
    other = other.reshape(cols, ROWS)
    n = NZ * ROWS
    work = dict(flops=6 * n * cols * ROWS, nbytes=2**20, exps=n * cols)
    scratch = (pltpu.VMEM((n, cols), BF16), pltpu.VMEM((n, cols), BF16), pltpu.VMEM((NZ, ROWS), F32))
    first = call(
        functools.partial(sums_kernel, True),
        [sds((NZ, ROWS)), sds((n, ROWS)), sds((n, ROWS))],
        scratch,
        **work,
    )(place, *rows, plane, mates)
    send, *ap = call(
        functools.partial(sums_kernel, False),
        [sds((NDEV, 1, 2 * ROWS))] + [sds((2 * ROWS, ROWS))] * NZ,
        scratch,
        **work,
    )(place, *rows, other, mates, *first)
    got = lax.all_to_all(send, ALL, 0, 0, tiled=True)
    ap = [ap[0]] + [shift(ap[r], -r) for r in range(1, NZ)]
    got, *ap = lax.optimization_barrier((got, *ap))
    *b, aux = call(
        grads_kernel,
        [sds((ROWS + 8, ROWS))] * NZ + [sds((8, ROWS))],
        (pltpu.VMEM((NCO, 1, cols), F32), pltpu.VMEM((NCO, n, cols), BF16)),
        flops=8 * n * cols * ROWS,
        nbytes=2**20,
        exps=2 * n * cols,
    )(place, *rows, plane, other, got)
    b = [b[0]] + [shift(b[r], -r) for r in range(1, NZ)]
    loss, grad = call(
        final_kernel,
        [sds((1, 1)), sds((ROWS, ROWS))],
        (pltpu.VMEM((NZ, 8, ROWS), F32),),
    )(place, proj, aux, *ap, *b)
    return loss.reshape(()), grad


def solution(mesh):
    fine = Mesh(mesh.devices.reshape(4, 2, 2, 4, 2), ALL)
    return jax.shard_map(
        body,
        mesh=fine,
        in_specs=(P(ALL, None), P()),
        out_specs=(P(), P(ALL, None)),
        check_vma=False,
    )
```

```python
import functools
import math

import jax
import jax.numpy as jnp
from jax import lax
from jax.experimental import pallas as pl
from jax.experimental.pallas import tpu as pltpu
from jax.sharding import Mesh, PartitionSpec as P

EPS = 1e-06
INV_TEMP = 10.0
SCALE = INV_TEMP * math.log2(math.e)

ROWS = 128
NXY = 16
NZ = 4
NCO = 2
NDEV = NXY * NZ * NCO
VIEWS = NDEV * ROWS
XY = ("y", "xh", "xl")
ALL = ("y", "xh", "xl", "z", "co")
CHUNK = 256
F32 = jnp.float32
BF16 = jnp.bfloat16
VMEM = pl.BlockSpec(memory_space=pltpu.VMEM)
SMEM = pl.BlockSpec(memory_space=pltpu.SMEM)


def call(body, outs, scratch=(), flops=0, nbytes=0, exps=0):
    def run(*args):
        return pl.pallas_call(
            body,
            out_shape=outs,
            in_specs=[SMEM if a.dtype == jnp.int32 and a.ndim == 1 else VMEM for a in args],
            out_specs=[VMEM] * len(outs),
            scratch_shapes=list(scratch),
            compiler_params=pltpu.CompilerParams(vmem_limit_bytes=24 * 2**20),
            cost_estimate=pl.CostEstimate(flops=flops, bytes_accessed=nbytes, transcendentals=exps),
        )(*args)

    return run


def sds(shape, dtype=F32):
    return jax.ShapeDtypeStruct(shape, dtype)


def dot_nt(a, b):
    return lax.dot_general(a, b, (((1,), (1,)), ((), ())), preferred_element_type=F32)


def dot_nn(a, b):
    return lax.dot_general(a, b, (((1,), (0,)), ((), ())), preferred_element_type=F32)


def down_rows(row):
    return jnp.transpose(jnp.broadcast_to(row, (ROWS, ROWS)))


def norm_kernel(x_ref, u_ref, copies_ref):
    x = x_ref[...]
    radius = jnp.sqrt(jnp.sum(x * x, axis=1, keepdims=True) + EPS)
    unit = (x / radius).astype(BF16)
    u_ref[...] = unit
    copies_ref[...] = jnp.broadcast_to(unit[None], (NXY, ROWS, ROWS))


def expo(s):
    return jnp.exp2(s * SCALE)


def local_mates(mates, z, half):
    here = (((mates >> 8) & 3) == z) & (((mates >> 7) & 1) == half)
    return jnp.where(here, ((mates >> 10) << 7) | (mates & 127), -1)


def sums_kernel(own_half, *refs):
    place_ref, u0, u1, u2, u3, c_ref, mate_ref = refs[:7]
    z, co, xy = place_ref[0], place_ref[1], place_ref[2]
    half = co if own_half else 1 - co
    mates = mate_ref[...]
    local = local_mates(mates, z, half)
    width = NZ * ROWS
    mate = jnp.concatenate([local[r : r + 1] for r in range(NZ)], axis=1)
    mate = jnp.broadcast_to(mate, (8, width))
    u = jnp.concatenate([u0[...], u1[...], u2[...], u3[...]], axis=0)
    down = lax.broadcasted_iota(jnp.int32, (8, width), 0)
    sums = jnp.zeros((8, width), F32)
    pos = jnp.zeros((8, width), F32)
    for c in range(0, c_ref.shape[0], CHUNK):
        s = dot_nt(c_ref[c : c + CHUNK], u)
        e = expo(s)
        if own_half:
            col = lax.broadcasted_iota(jnp.int32, (CHUNK, ROWS), 0) + (c - xy * ROWS)
            row = lax.broadcasted_iota(jnp.int32, (CHUNK, ROWS), 1)
            e = jnp.concatenate([jnp.where(col == row, 0.0, e[:, :ROWS]), e[:, ROWS:]], axis=1)
        for k in range(0, CHUNK, 8):
            sums = sums + e[k : k + 8]
            pos = pos + jnp.where(mate == down + (c + k), s[k : k + 8], 0.0)
    sums = jnp.sum(sums, axis=0, keepdims=True)
    pos = jnp.sum(pos, axis=0, keepdims=True) * INV_TEMP
    rows = [sums[:, r * ROWS : (r + 1) * ROWS] for r in range(NZ)]
    rows.append(sum(pos[:, r * ROWS : (r + 1) * ROWS] for r in range(NZ)))
    if own_half:
        out_ref = refs[7]
        for q, row in enumerate(rows):
            out_ref[q : q + 1] = row
        out_ref[5:8] = jnp.zeros((3, ROWS), F32)
        return
    in_ref, send_ref, out_ref = refs[7:]
    rows = [row + in_ref[q : q + 1] for q, row in enumerate(rows)]
    for q in range(NZ):
        out_ref[q : q + 1] = rows[q]
    out_ref[4:8] = jnp.zeros((4, ROWS), F32)
    for k in range(NZ):
        r = lax.rem(k - z + NZ, NZ)
        row = rows[0]
        for q in range(1, NZ):
            row = jnp.where(r == q, rows[q], row)
        piece = jnp.concatenate([row, rows[NZ]], axis=1)
        for xy_to in range(NXY):
            for co_to in range(NCO):
                send_ref[xy_to * 8 + k * 2 + co_to] = piece


def grads_kernel(
    place_ref, u0, u1, u2, u3, own_ref, other_ref, mate_ref, got_ref, s0, s1, s2, s3, b0, b1, b2, b3, aux_ref, inv_ref
):
    z, co, xy = place_ref[0], place_ref[1], place_ref[2]
    logs = jnp.zeros((1, ROWS), F32)
    for k in range(NXY):
        for c in range(NCO):
            total = got_ref[k * 8 + c, :, 0:ROWS]
            for q in range(1, NZ):
                total = total + got_ref[k * 8 + q * 2 + c, :, 0:ROWS]
            logs = logs + jnp.log(total)
            inv_ref[c, :, k * ROWS : (k + 1) * ROWS] = 1.0 / total
    pos = got_ref[0, :, ROWS:]
    for k in range(1, NDEV):
        pos = pos + got_ref[k, :, ROWS:]
    aux_ref[0:1] = pos
    aux_ref[1:8] = jnp.zeros((7, ROWS), F32)
    parts = (s0, s1, s2, s3)
    inv_row = []
    for r in range(NZ):
        total = s0[r : r + 1]
        for q in range(1, NZ):
            k = (r - q) % NZ
            total = total + parts[q][k : k + 1]
        inv_row.append(down_rows(1.0 / total))
    inv_row = jnp.concatenate(inv_row, axis=0)
    mates = mate_ref[...]
    u = jnp.concatenate([u0[...], u1[...], u2[...], u3[...]], axis=0)
    lane = lax.broadcasted_iota(jnp.int32, (NZ * ROWS, ROWS), 1)
    total = jnp.zeros((NZ * ROWS, ROWS), F32)
    for h, c_ref in enumerate((own_ref, other_ref)):
        half = co if h == 0 else 1 - co
        local = local_mates(mates, z, half)
        mate = jnp.concatenate([down_rows(local[r : r + 1]) for r in range(NZ)], axis=0)
        for c in range(0, c_ref.shape[0], CHUNK):
            e = expo(dot_nt(u, c_ref[c : c + CHUNK]))
            if h == 0:
                col = lax.broadcasted_iota(jnp.int32, (ROWS, CHUNK), 1) + (c - xy * ROWS)
                row = lax.broadcasted_iota(jnp.int32, (ROWS, CHUNK), 0)
                e = jnp.concatenate([jnp.where(col == row, 0.0, e[:ROWS]), e[ROWS:]], axis=0)
            weight = []
            for k in range(0, CHUNK, ROWS):
                w = e[:, k : k + ROWS] * (inv_row + inv_ref[half, :, c + k : c + k + ROWS])
                w = w - jnp.where(mate == lane + (c + k), 2.0, 0.0)
                weight.append(w.astype(BF16))
            total = total + dot_nn(jnp.concatenate(weight, axis=1), c_ref[c : c + CHUNK])
    for r, b_ref in enumerate((b0, b1, b2, b3)):
        b_ref[0:ROWS] = total[r * ROWS : (r + 1) * ROWS]
        b_ref[ROWS : ROWS + 1] = logs
        b_ref[ROWS + 1 :] = jnp.zeros((7, ROWS), F32)


def final_kernel(place_ref, x_ref, aux_ref, b0, b1, b2, b3, loss_ref, grad_ref, log_ref):
    z = place_ref[0]
    x = x_ref[...]
    radius = jnp.sqrt(jnp.sum(x * x, axis=1, keepdims=True) + EPS)
    unit = x / radius
    d = INV_TEMP * (b0[0:ROWS] + b1[0:ROWS] + b2[0:ROWS] + b3[0:ROWS])
    grad_ref[...] = (d - unit * jnp.sum(unit * d, axis=1, keepdims=True)) / radius
    for r, b_ref in enumerate((b0, b1, b2, b3)):
        log_ref[lax.rem(z - r + NZ, NZ)] = b_ref[ROWS : ROWS + 8]
    logs = log_ref[0, 0:1]
    for k in range(1, NZ):
        logs = logs + log_ref[k, 0:1]
    loss_ref[...] = jnp.sum(logs - aux_ref[0:1], axis=1, keepdims=True) / VIEWS


def shift(x, by):
    return lax.ppermute(x, "z", [((k + by) % NZ, k) for k in range(NZ)])


def body(proj, partner):
    y, xh, xl = (lax.axis_index(a) for a in XY)
    z, co = lax.axis_index("z"), lax.axis_index("co")
    xy = (y * 2 + xh) * 2 + xl
    place = jnp.stack([z, co, xy]).astype(jnp.int32)
    unit, copies = call(norm_kernel, [sds((ROWS, ROWS), BF16), sds((NXY, ROWS, ROWS), BF16)])(proj)
    plane = lax.all_to_all(copies, XY, 0, 0, tiled=True)
    rows = [unit] + [shift(unit, r) for r in range(1, NZ)]
    mates = partner.reshape(NXY, NZ, NCO, ROWS)
    mates = lax.dynamic_slice(mates, (xy, 0, co, 0), (1, NZ, 1, ROWS)).reshape(NZ, ROWS)
    mates = jnp.concatenate([mates, mates])
    mates = lax.dynamic_slice_in_dim(mates, z, NZ, 0)
    plane, mates, *rows = lax.optimization_barrier((plane, mates, *rows))
    other = lax.ppermute(plane, "co", [(0, 1), (1, 0)])
    cols = NXY * ROWS
    plane = plane.reshape(cols, ROWS)
    other = other.reshape(cols, ROWS)
    n = NZ * ROWS
    work = dict(flops=2 * n * cols * ROWS, nbytes=2**20, exps=n * cols)
    first = call(
        functools.partial(sums_kernel, True), [sds((8, ROWS))], **work
    )(place, *rows, plane, mates)
    send, sums = call(
        functools.partial(sums_kernel, False),
        [sds((NDEV, 1, 2 * ROWS)), sds((8, ROWS))],
        **work,
    )(place, *rows, other, mates, *first)
    got = lax.all_to_all(send, ALL, 0, 0, tiled=True)
    sums = [sums] + [shift(sums, r) for r in range(1, NZ)]
    got, *sums = lax.optimization_barrier((got, *sums))
    *b, aux = call(
        grads_kernel,
        [sds((ROWS + 8, ROWS))] * NZ + [sds((8, ROWS))],
        (pltpu.VMEM((NCO, 1, cols), F32),),
        flops=8 * n * cols * ROWS,
        nbytes=2**20,
        exps=2 * n * cols,
    )(place, *rows, plane, other, mates, got, *sums)
    b = [b[0]] + [shift(b[r], -r) for r in range(1, NZ)]
    loss, grad = call(
        final_kernel,
        [sds((1, 1)), sds((ROWS, ROWS))],
        (pltpu.VMEM((NZ, 8, ROWS), F32),),
    )(place, proj, aux, *b)
    return loss.reshape(()), grad


def solution(mesh):
    fine = Mesh(mesh.devices.reshape(4, 2, 2, 4, 2), ALL)
    return jax.shard_map(
        body,
        mesh=fine,
        in_specs=(P(ALL, None), P()),
        out_specs=(P(), P(ALL, None)),
        check_vma=False,
    )
```

```python
import functools
import math

import jax
import jax.numpy as jnp
from jax import lax
from jax.experimental import pallas as pl
from jax.experimental.pallas import tpu as pltpu
from jax.sharding import Mesh, PartitionSpec as P

EPS = 1e-06
INV_TEMP = 10.0
SCALE = INV_TEMP * math.log2(math.e)

ROWS = 128
NXY = 16
NZ = 4
NCO = 2
NDEV = NXY * NZ * NCO
VIEWS = NDEV * ROWS
XY = ("y", "xh", "xl")
ALL = ("y", "xh", "xl", "z", "co")
CHUNK = 256
F32 = jnp.float32
BF16 = jnp.bfloat16
VMEM = pl.BlockSpec(memory_space=pltpu.VMEM)
SMEM = pl.BlockSpec(memory_space=pltpu.SMEM)


def call(body, outs, scratch=(), flops=0, nbytes=0, exps=0):
    def run(*args):
        return pl.pallas_call(
            body,
            out_shape=outs,
            in_specs=[SMEM if a.dtype == jnp.int32 and a.ndim == 1 else VMEM for a in args],
            out_specs=[VMEM] * len(outs),
            scratch_shapes=list(scratch),
            compiler_params=pltpu.CompilerParams(vmem_limit_bytes=16 * 2**20),
            cost_estimate=pl.CostEstimate(flops=flops, bytes_accessed=nbytes, transcendentals=exps),
        )(*args)

    return run


def sds(shape, dtype=F32):
    return jax.ShapeDtypeStruct(shape, dtype)


def dot_nt(a, b):
    return lax.dot_general(a, b, (((1,), (1,)), ((), ())), preferred_element_type=F32)


def dot_nn(a, b):
    return lax.dot_general(a, b, (((1,), (0,)), ((), ())), preferred_element_type=F32)


def down_rows(row):
    return jnp.transpose(jnp.broadcast_to(row, (ROWS, ROWS)))


def norm_kernel(x_ref, u_ref, copies_ref):
    x = x_ref[...]
    radius = jnp.sqrt(jnp.sum(x * x, axis=1, keepdims=True) + EPS)
    unit = (x / radius).astype(BF16)
    u_ref[...] = unit
    copies_ref[...] = jnp.broadcast_to(unit[None], (NXY, ROWS, ROWS))


def expo(s):
    return jnp.exp2(s * SCALE)


def local_mates(mates, z, half):
    here = (((mates >> 8) & 3) == z) & (((mates >> 7) & 1) == half)
    return jnp.where(here, ((mates >> 10) << 7) | (mates & 127), -1)


def sums_kernel(own_half, *refs):
    place_ref, u0, u1, u2, u3, c_ref, mate_ref = refs[:7]
    z, co, xy = place_ref[0], place_ref[1], place_ref[2]
    half = co if own_half else 1 - co
    mates = mate_ref[...]
    here = local_mates(mates, z, half)
    width = 2 * ROWS
    down = lax.broadcasted_iota(jnp.int32, (8, width), 0)
    sums, pos = [], jnp.zeros((8, width), F32)
    for g in range(0, NZ, 2):
        u = jnp.concatenate([ref[...] for ref in (u0, u1, u2, u3)[g : g + 2]], axis=0)
        mate = jnp.broadcast_to(jnp.concatenate([here[g : g + 1], here[g + 1 : g + 2]], axis=1), (8, width))
        block = mate >> 7
        total = jnp.zeros((8, width), F32)
        kept = [jnp.zeros((8, width), F32)] * (ROWS // 8)
        for c in range(0, c_ref.shape[0], CHUNK):
            s = dot_nt(c_ref[c : c + CHUNK], u)
            for k in range(0, CHUNK, 8):
                q = k % ROWS // 8
                kept[q] = jnp.where(block == (c + k) // ROWS, s[k : k + 8], kept[q])
            e = expo(s)
            if own_half and g == 0:
                col = lax.broadcasted_iota(jnp.int32, (CHUNK, ROWS), 0) + (c - xy * ROWS)
                row = lax.broadcasted_iota(jnp.int32, (CHUNK, ROWS), 1)
                e = jnp.concatenate([jnp.where(col == row, 0.0, e[:, :ROWS]), e[:, ROWS:]], axis=1)
            for k in range(0, CHUNK, 8):
                total = total + e[k : k + 8]
        for q, s in enumerate(kept):
            pos = pos + jnp.where((mate & 127) == down + 8 * q, s, 0.0)
        sums.append(jnp.sum(total, axis=0, keepdims=True))
    sums = jnp.concatenate(sums, axis=1)
    pos = jnp.sum(pos, axis=0, keepdims=True) * INV_TEMP
    rows = [sums[:, r * ROWS : (r + 1) * ROWS] for r in range(NZ)]
    rows.append(pos[:, :ROWS] + pos[:, ROWS:])
    if own_half:
        out_ref = refs[7]
        for q, row in enumerate(rows):
            out_ref[q : q + 1] = row
        out_ref[5:8] = jnp.zeros((3, ROWS), F32)
        return
    in_ref, send_ref = refs[7:]
    rows = [row + in_ref[q : q + 1] for q, row in enumerate(rows)]
    planes = []
    for k in range(NZ):
        r = lax.rem(k - z + NZ, NZ)
        row = rows[0]
        for q in range(1, NZ):
            row = jnp.where(r == q, rows[q], row)
        planes.append(row)
    pos = rows[NZ]
    high = pos.astype(BF16).astype(F32)
    for k in range(NZ):
        q = [planes[(k + r) % NZ] for r in range(NZ)]
        top = jnp.concatenate([q[0], q[1], high], axis=1)
        low = jnp.concatenate([q[2], q[3], pos - high], axis=1)
        piece = jnp.concatenate([top, low], axis=0).astype(BF16)
        for xy_to in range(NXY):
            for co_to in range(NCO):
                send_ref[xy_to * 8 + k * 2 + co_to] = piece


def grads_kernel(blocks, *refs):
    n = len(blocks)
    first = 0 not in blocks
    place_ref, own_ref, other_ref, mate_ref = refs[:4]
    u_refs = refs[4 : 4 + n]
    z, co, xy = place_ref[0], place_ref[1], place_ref[2]
    got_ref = refs[4 + n]
    if first:
        out_refs = refs[5 + n : 5 + 2 * n]
        inv_ref, aux_ref = refs[5 + 2 * n :]
        for k in range(NXY):
            for c in range(NCO):
                got = [got_ref[k * 8 + q * 2 + c, :, 0:ROWS].astype(F32) for q in range(NZ)]
                total = got[0] + got[1] + (got[2] + got[3])
                inv_ref[c, :, k * ROWS : (k + 1) * ROWS] = 1.0 / total[0:1]
        got = [got_ref[xy * 8 + q * 2 + co, :, 0 : 2 * ROWS].astype(F32) for q in range(NZ)]
        total = got[0] + got[1] + (got[2] + got[3])
        for r in range(NZ):
            part = total[r // 2 : r // 2 + 1, r % 2 * ROWS : (r % 2 + 1) * ROWS]
            aux_ref[r : r + 1] = 1.0 / part
        aux_ref[NZ:] = jnp.zeros((8 - NZ, ROWS), F32)
    else:
        inv_ref, aux_ref, *out_refs, loss_ref = refs[5 + n :]
        logs = jnp.zeros((2, 2 * ROWS), F32)
        pos = jnp.zeros((2, ROWS), F32)
        for k in range(NXY):
            for c in range(NCO):
                got = [got_ref[k * 8 + q * 2 + c].astype(F32) for q in range(NZ)]
                got = got[0] + got[1] + (got[2] + got[3])
                pos = pos + got[:, 2 * ROWS :]
                logs = logs + jnp.log(got[:, : 2 * ROWS])
        pos = jnp.sum(pos, axis=0, keepdims=True)
        parts = [logs[r // 2 : r // 2 + 1, r % 2 * ROWS : (r % 2 + 1) * ROWS] for r in range(NZ)]
        loss = -pos
        for k in range(NZ):
            r = lax.rem(k - z + NZ, NZ)
            row = parts[0]
            for q in range(1, NZ):
                row = jnp.where(r == q, parts[q], row)
            loss = loss + row
        loss_ref[...] = jnp.sum(loss, axis=1, keepdims=True) / VIEWS
    inv_row = jnp.concatenate([down_rows(aux_ref[r : r + 1]) for r in blocks], axis=0)
    mates = mate_ref[...]
    u = jnp.concatenate([ref[...] for ref in u_refs], axis=0)
    lane = lax.broadcasted_iota(jnp.int32, (n * ROWS, ROWS), 1)
    total = jnp.zeros((n * ROWS, ROWS), F32)
    for h, c_ref in enumerate((own_ref, other_ref)):
        half = co if h == 0 else 1 - co
        local = local_mates(mates, z, half)
        mate = jnp.concatenate([down_rows(local[r : r + 1]) for r in blocks], axis=0)
        for c in range(0, c_ref.shape[0], CHUNK):
            e = expo(dot_nt(u, c_ref[c : c + CHUNK]))
            if h == 0 and not first:
                col = lax.broadcasted_iota(jnp.int32, e.shape, 1) + (c - xy * ROWS)
                row = lax.broadcasted_iota(jnp.int32, e.shape, 0)
                e = jnp.where(col == row, 0.0, e)
            weight = []
            for k in range(0, CHUNK, ROWS):
                w = e[:, k : k + ROWS] * (inv_row + inv_ref[half, :, c + k : c + k + ROWS])
                w = w - jnp.where(mate == lane + (c + k), 2.0, 0.0)
                weight.append(w.astype(BF16))
            total = total + dot_nn(jnp.concatenate(weight, axis=1), c_ref[c : c + CHUNK])
    for q, out_ref in enumerate(out_refs):
        out_ref[...] = total[q * ROWS : (q + 1) * ROWS]


def final_kernel(x_ref, b0, b1, b2, b3, grad_ref):
    x = x_ref[...]
    radius = jnp.sqrt(jnp.sum(x * x, axis=1, keepdims=True) + EPS)
    unit = x / radius
    d = INV_TEMP * (b0[...] + b1[...] + b2[...] + b3[...])
    grad_ref[...] = (d - unit * jnp.sum(unit * d, axis=1, keepdims=True)) / radius


def shift(x, by):
    return lax.ppermute(x, "z", [((k + by) % NZ, k) for k in range(NZ)])


def body(proj, partner):
    y, xh, xl = (lax.axis_index(a) for a in XY)
    z, co = lax.axis_index("z"), lax.axis_index("co")
    xy = (y * 2 + xh) * 2 + xl
    place = jnp.stack([z, co, xy]).astype(jnp.int32)
    unit, copies = call(norm_kernel, [sds((ROWS, ROWS), BF16), sds((NXY, ROWS, ROWS), BF16)])(proj)
    plane = lax.all_to_all(copies, XY, 0, 0, tiled=True)
    rows = [unit] + [shift(unit, r) for r in range(1, NZ)]
    mates = partner.reshape(NXY, NZ, NCO, ROWS)
    mates = lax.dynamic_slice(mates, (xy, 0, co, 0), (1, NZ, 1, ROWS)).reshape(NZ, ROWS)
    mates = jnp.concatenate([mates, mates])
    mates = lax.dynamic_slice_in_dim(mates, z, NZ, 0)
    plane, mates, *rows = lax.optimization_barrier((plane, mates, *rows))
    other = lax.ppermute(plane, "co", [(0, 1), (1, 0)])
    cols = NXY * ROWS
    plane = plane.reshape(cols, ROWS)
    other = other.reshape(cols, ROWS)
    n = NZ * ROWS
    work = dict(flops=2 * n * cols * ROWS, nbytes=2**20, exps=n * cols)
    first = call(
        functools.partial(sums_kernel, True), [sds((8, ROWS))], **work
    )(place, *rows, plane, mates)
    (send,) = call(
        functools.partial(sums_kernel, False), [sds((NDEV, 2, 3 * ROWS), BF16)], **work
    )(place, *rows, other, mates, *first)
    got = lax.all_to_all(send, ALL, 0, 0, tiled=True)
    work = dict(flops=6 * n * cols * ROWS, nbytes=2**20, exps=2 * n * cols)
    block = sds((ROWS, ROWS))
    held = (place, plane, other, mates)
    b1, b2, b3, *inv = call(
        functools.partial(grads_kernel, (1, 2, 3)),
        [block] * 3 + [sds((NCO, 1, cols)), sds((8, ROWS))],
        **work,
    )(*held, *rows[1:], got)
    b0, loss = call(functools.partial(grads_kernel, (0,)), [block, sds((1, 1))], **work)(*held, rows[0], got, *inv)
    b = [b0, shift(b1, -1), shift(b2, -2), shift(b3, -3)]
    (grad,) = call(final_kernel, [sds((ROWS, ROWS))])(proj, *b)
    return loss.reshape(()), grad


def solution(mesh):
    fine = Mesh(mesh.devices.reshape(4, 2, 2, 4, 2), ALL)
    return jax.shard_map(
        body,
        mesh=fine,
        in_specs=(P(ALL, None), P()),
        out_specs=(P(), P(ALL, None)),
        check_vma=False,
    )
```

```python
import functools
import math

import jax
import jax.numpy as jnp
from jax import lax
from jax.experimental import pallas as pl
from jax.experimental.pallas import tpu as pltpu
from jax.sharding import Mesh, PartitionSpec as P

EPS = 1e-06
INV_TEMP = 10.0
SCALE = INV_TEMP * math.log2(math.e)

ROWS = 128
NXY = 16
NZ = 4
NCO = 2
NDEV = NXY * NZ * NCO
VIEWS = NDEV * ROWS
XY = ("y", "xh", "xl")
ALL = ("y", "xh", "xl", "z", "co")
FIRST = (10, 5)
PLANES = [
    [(FIRST[c] + k) % NXY * 8 + z * 2 + c for k in range(NXY)] for z in range(NZ) for c in range(NCO)
]
CHUNK = 256
F32 = jnp.float32
BF16 = jnp.bfloat16
VMEM = pl.BlockSpec(memory_space=pltpu.VMEM)
SMEM = pl.BlockSpec(memory_space=pltpu.SMEM)


def call(body, outs, scratch=(), flops=0, nbytes=0, exps=0):
    def run(*args):
        return pl.pallas_call(
            body,
            out_shape=outs,
            in_specs=[SMEM if a.dtype == jnp.int32 and a.ndim == 1 else VMEM for a in args],
            out_specs=[VMEM] * len(outs),
            scratch_shapes=list(scratch),
            compiler_params=pltpu.CompilerParams(vmem_limit_bytes=16 * 2**20),
            cost_estimate=pl.CostEstimate(flops=flops, bytes_accessed=nbytes, transcendentals=exps),
        )(*args)

    return run


def sds(shape, dtype=F32):
    return jax.ShapeDtypeStruct(shape, dtype)


def dot_nt(a, b):
    return lax.dot_general(a, b, (((1,), (1,)), ((), ())), preferred_element_type=F32)


def dot_nn(a, b):
    return lax.dot_general(a, b, (((1,), (0,)), ((), ())), preferred_element_type=F32)


def down_rows(row):
    return jnp.transpose(jnp.broadcast_to(row, (ROWS, ROWS)))


def norm_kernel(x_ref, u_ref, copies_ref):
    x = x_ref[...]
    radius = jnp.sqrt(jnp.sum(x * x, axis=1, keepdims=True) + EPS)
    unit = (x / radius).astype(BF16)
    u_ref[...] = unit
    copies_ref[...] = jnp.broadcast_to(unit[None], (NXY, ROWS, ROWS))


def expo(s):
    return jnp.exp2(s * SCALE)


def slot(xy, half):
    return (xy - FIRST[0] + (FIRST[0] - FIRST[1]) * half) & (NXY - 1)


def local_mates(mates, z, half):
    here = (((mates >> 8) & 3) == z) & (((mates >> 7) & 1) == half)
    return jnp.where(here, (slot(mates >> 10, half) << 7) | (mates & 127), -1)


def sums_kernel(own_half, *refs):
    place_ref, u0, u1, u2, u3, c_ref, mate_ref = refs[:7]
    z, co, xy = place_ref[0], place_ref[1], place_ref[2]
    half = co if own_half else 1 - co
    mates = mate_ref[...]
    here = local_mates(mates, z, half)
    own = slot(xy, co)
    width = 2 * ROWS
    down = lax.broadcasted_iota(jnp.int32, (8, width), 0)
    sums, pos = [], jnp.zeros((8, width), F32)
    for g in range(0, NZ, 2):
        u = jnp.concatenate([ref[...] for ref in (u0, u1, u2, u3)[g : g + 2]], axis=0)
        mate = jnp.broadcast_to(jnp.concatenate([here[g : g + 1], here[g + 1 : g + 2]], axis=1), (8, width))
        block = mate >> 7
        total = jnp.zeros((8, width), F32)
        kept = [jnp.zeros((8, width), F32)] * (ROWS // 8)
        for c in range(0, c_ref.shape[0], CHUNK):
            s = dot_nt(c_ref[c : c + CHUNK], u)
            for k in range(0, CHUNK, 8):
                q = k % ROWS // 8
                kept[q] = jnp.where(block == (c + k) // ROWS, s[k : k + 8], kept[q])
            e = expo(s)
            if own_half and g == 0:
                col = lax.broadcasted_iota(jnp.int32, (CHUNK, ROWS), 0) + (c - own * ROWS)
                row = lax.broadcasted_iota(jnp.int32, (CHUNK, ROWS), 1)
                e = jnp.concatenate([jnp.where(col == row, 0.0, e[:, :ROWS]), e[:, ROWS:]], axis=1)
            for k in range(0, CHUNK, 8):
                total = total + e[k : k + 8]
        for q, s in enumerate(kept):
            pos = pos + jnp.where((mate & 127) == down + 8 * q, s, 0.0)
        sums.append(jnp.sum(total, axis=0, keepdims=True))
    sums = jnp.concatenate(sums, axis=1)
    pos = jnp.sum(pos, axis=0, keepdims=True) * INV_TEMP
    rows = [sums[:, r * ROWS : (r + 1) * ROWS] for r in range(NZ)]
    rows.append(pos[:, :ROWS] + pos[:, ROWS:])
    if own_half:
        out_ref = refs[7]
        for q, row in enumerate(rows):
            out_ref[q : q + 1] = row
        out_ref[5:8] = jnp.zeros((3, ROWS), F32)
        return
    in_ref, send_ref = refs[7:]
    rows = [row + in_ref[q : q + 1] for q, row in enumerate(rows)]
    planes = []
    for k in range(NZ):
        r = lax.rem(k - z + NZ, NZ)
        row = rows[0]
        for q in range(1, NZ):
            row = jnp.where(r == q, rows[q], row)
        planes.append(row)
    pos = rows[NZ]
    high = pos.astype(BF16).astype(F32)
    for k in range(NZ):
        q = [planes[(k + r) % NZ] for r in range(NZ)]
        top = jnp.concatenate([q[0], q[1], high], axis=1)
        low = jnp.concatenate([q[2], q[3], pos - high], axis=1)
        piece = jnp.concatenate([top, low], axis=0).astype(BF16)
        for xy_to in range(NXY):
            for co_to in range(NCO):
                send_ref[xy_to * 8 + k * 2 + co_to] = piece


def grads_kernel(blocks, *refs):
    n = len(blocks)
    first = 0 not in blocks
    place_ref, own_ref, other_ref, mate_ref = refs[:4]
    u_refs = refs[4 : 4 + n]
    z, co, xy = place_ref[0], place_ref[1], place_ref[2]
    got_ref = refs[4 + n]
    if first:
        out_refs = refs[5 + n : 5 + 2 * n]
        inv_ref, aux_ref = refs[5 + 2 * n :]
        for k in range(NXY):
            for c in range(NCO):
                got = [got_ref[k * 8 + q * 2 + c, :, 0:ROWS].astype(F32) for q in range(NZ)]
                total = got[0] + got[1] + (got[2] + got[3])
                at = slot(k, c) * ROWS
                inv_ref[c, :, at : at + ROWS] = 1.0 / total[0:1]
        got = [got_ref[xy * 8 + q * 2 + co, :, 0 : 2 * ROWS].astype(F32) for q in range(NZ)]
        total = got[0] + got[1] + (got[2] + got[3])
        for r in range(NZ):
            part = total[r // 2 : r // 2 + 1, r % 2 * ROWS : (r % 2 + 1) * ROWS]
            aux_ref[r : r + 1] = 1.0 / part
        aux_ref[NZ:] = jnp.zeros((8 - NZ, ROWS), F32)
    else:
        inv_ref, aux_ref, *out_refs, loss_ref = refs[5 + n :]
        logs = jnp.zeros((2, 2 * ROWS), F32)
        pos = jnp.zeros((2, ROWS), F32)
        for k in range(NXY):
            for c in range(NCO):
                got = [got_ref[k * 8 + q * 2 + c].astype(F32) for q in range(NZ)]
                got = got[0] + got[1] + (got[2] + got[3])
                pos = pos + got[:, 2 * ROWS :]
                logs = logs + jnp.log(got[:, : 2 * ROWS])
        pos = jnp.sum(pos, axis=0, keepdims=True)
        parts = [logs[r // 2 : r // 2 + 1, r % 2 * ROWS : (r % 2 + 1) * ROWS] for r in range(NZ)]
        loss = -pos
        for k in range(NZ):
            r = lax.rem(k - z + NZ, NZ)
            row = parts[0]
            for q in range(1, NZ):
                row = jnp.where(r == q, parts[q], row)
            loss = loss + row
        loss_ref[...] = jnp.sum(loss, axis=1, keepdims=True) / VIEWS
    own = slot(xy, co)
    inv_row = jnp.concatenate([down_rows(aux_ref[r : r + 1]) for r in blocks], axis=0)
    mates = mate_ref[...]
    u = jnp.concatenate([ref[...] for ref in u_refs], axis=0)
    lane = lax.broadcasted_iota(jnp.int32, (n * ROWS, ROWS), 1)
    total = jnp.zeros((n * ROWS, ROWS), F32)
    for h, c_ref in enumerate((own_ref, other_ref)):
        half = co if h == 0 else 1 - co
        local = local_mates(mates, z, half)
        mate = jnp.concatenate([down_rows(local[r : r + 1]) for r in blocks], axis=0)
        for c in range(0, c_ref.shape[0], CHUNK):
            e = expo(dot_nt(u, c_ref[c : c + CHUNK]))
            if h == 0 and not first:
                col = lax.broadcasted_iota(jnp.int32, e.shape, 1) + (c - own * ROWS)
                row = lax.broadcasted_iota(jnp.int32, e.shape, 0)
                e = jnp.where(col == row, 0.0, e)
            weight = []
            for k in range(0, CHUNK, ROWS):
                w = e[:, k : k + ROWS] * (inv_row + inv_ref[half, :, c + k : c + k + ROWS])
                w = w - jnp.where(mate == lane + (c + k), 2.0, 0.0)
                weight.append(w.astype(BF16))
            total = total + dot_nn(jnp.concatenate(weight, axis=1), c_ref[c : c + CHUNK])
    for q, out_ref in enumerate(out_refs):
        out_ref[...] = total[q * ROWS : (q + 1) * ROWS]


def final_kernel(x_ref, b0, b1, b2, b3, grad_ref):
    x = x_ref[...]
    radius = jnp.sqrt(jnp.sum(x * x, axis=1, keepdims=True) + EPS)
    unit = x / radius
    d = INV_TEMP * (b0[...] + b1[...] + b2[...] + b3[...])
    grad_ref[...] = (d - unit * jnp.sum(unit * d, axis=1, keepdims=True)) / radius


def shift(x, by):
    return lax.ppermute(x, "z", [((k + by) % NZ, k) for k in range(NZ)])


def body(proj, partner):
    y, xh, xl = (lax.axis_index(a) for a in XY)
    z, co = lax.axis_index("z"), lax.axis_index("co")
    xy = (y * 2 + xh) * 2 + xl
    place = jnp.stack([z, co, xy]).astype(jnp.int32)
    unit, copies = call(norm_kernel, [sds((ROWS, ROWS), BF16), sds((NXY, ROWS, ROWS), BF16)])(proj)
    plane = lax.all_to_all(copies, ALL, 0, 0, axis_index_groups=PLANES, tiled=True)
    rows = [unit] + [shift(unit, r) for r in range(1, NZ)]
    mates = partner.reshape(NXY, NZ, NCO, ROWS)
    mates = lax.dynamic_slice(mates, (xy, 0, co, 0), (1, NZ, 1, ROWS)).reshape(NZ, ROWS)
    mates = jnp.concatenate([mates, mates])
    mates = lax.dynamic_slice_in_dim(mates, z, NZ, 0)
    plane, mates, *rows = lax.optimization_barrier((plane, mates, *rows))
    other = lax.ppermute(plane, "co", [(0, 1), (1, 0)])
    cols = NXY * ROWS
    plane = plane.reshape(cols, ROWS)
    other = other.reshape(cols, ROWS)
    n = NZ * ROWS
    work = dict(flops=2 * n * cols * ROWS, nbytes=2**20, exps=n * cols)
    first = call(
        functools.partial(sums_kernel, True), [sds((8, ROWS))], **work
    )(place, *rows, plane, mates)
    (send,) = call(
        functools.partial(sums_kernel, False), [sds((NDEV, 2, 3 * ROWS), BF16)], **work
    )(place, *rows, other, mates, *first)
    got = lax.all_to_all(send, ALL, 0, 0, tiled=True)
    work = dict(flops=6 * n * cols * ROWS, nbytes=2**20, exps=2 * n * cols)
    block = sds((ROWS, ROWS))
    held = (place, plane, other, mates)
    b1, b2, b3, *inv = call(
        functools.partial(grads_kernel, (1, 2, 3)),
        [block] * 3 + [sds((NCO, 1, cols)), sds((8, ROWS))],
        **work,
    )(*held, *rows[1:], got)
    b0, loss = call(functools.partial(grads_kernel, (0,)), [block, sds((1, 1))], **work)(*held, rows[0], got, *inv)
    b = [b0, shift(b1, -1), shift(b2, -2), shift(b3, -3)]
    (grad,) = call(final_kernel, [sds((ROWS, ROWS))])(proj, *b)
    return loss.reshape(()), grad


def solution(mesh):
    fine = Mesh(mesh.devices.reshape(4, 2, 2, 4, 2), ALL)
    return jax.shard_map(
        body,
        mesh=fine,
        in_specs=(P(ALL, None), P()),
        out_specs=(P(), P(ALL, None)),
        check_vma=False,
    )
```

```python
import functools
import math

import jax
import jax.numpy as jnp
from jax import lax
from jax.experimental import pallas as pl
from jax.experimental.pallas import tpu as pltpu
from jax.sharding import Mesh, PartitionSpec as P

EPS = 1e-06
INV_TEMP = 10.0
SCALE = INV_TEMP * math.log2(math.e)

ROWS = 128
NXY = 16
NZ = 4
NCO = 2
NDEV = NXY * NZ * NCO
VIEWS = NDEV * ROWS
XY = ("y", "xh", "xl")
ALL = ("y", "xh", "xl", "z", "co")
FIRST = (13, 5)
PLANES = [
    [(FIRST[c] + k) % NXY * 8 + z * 2 + c for k in range(NXY)] for z in range(NZ) for c in range(NCO)
]
CHUNK = 256
STRIP = 128
F32 = jnp.float32
BF16 = jnp.bfloat16
VMEM = pl.BlockSpec(memory_space=pltpu.VMEM)
SMEM = pl.BlockSpec(memory_space=pltpu.SMEM)


def call(body, outs, scratch=(), flops=0, nbytes=0, exps=0):
    def run(*args):
        return pl.pallas_call(
            body,
            out_shape=outs,
            in_specs=[SMEM if a.dtype == jnp.int32 and a.ndim == 1 else VMEM for a in args],
            out_specs=[VMEM] * len(outs),
            scratch_shapes=list(scratch),
            compiler_params=pltpu.CompilerParams(vmem_limit_bytes=16 * 2**20),
            cost_estimate=pl.CostEstimate(flops=flops, bytes_accessed=nbytes, transcendentals=exps),
        )(*args)

    return run


def sds(shape, dtype=F32):
    return jax.ShapeDtypeStruct(shape, dtype)


def dot_nt(a, b):
    return lax.dot_general(a, b, (((1,), (1,)), ((), ())), preferred_element_type=F32)


def dot_nn(a, b):
    return lax.dot_general(a, b, (((1,), (0,)), ((), ())), preferred_element_type=F32)


def down_rows(row):
    return jnp.transpose(jnp.broadcast_to(row, (ROWS, ROWS)))


def norm_kernel(x_ref, u_ref, copies_ref):
    x = x_ref[...]
    radius = jnp.sqrt(jnp.sum(x * x, axis=1, keepdims=True) + EPS)
    unit = (x / radius).astype(BF16)
    u_ref[...] = unit
    copies_ref[...] = jnp.broadcast_to(unit[None], (NXY, ROWS, ROWS))


def expo(s):
    return jnp.exp2(s * SCALE)


def slot(xy, half):
    return (xy - FIRST[0] + (FIRST[0] - FIRST[1]) * half) & (NXY - 1)


def local_mates(mates, z, half):
    here = (((mates >> 8) & 3) == z) & (((mates >> 7) & 1) == half)
    return jnp.where(here, (slot(mates >> 10, half) << 7) | (mates & 127), -1)


def sums_kernel(own_half, *refs):
    place_ref, u0, u1, u2, u3, c_ref, mate_ref = refs[:7]
    z, co, xy = place_ref[0], place_ref[1], place_ref[2]
    half = co if own_half else 1 - co
    mates = mate_ref[...]
    here = local_mates(mates, z, half)
    own = slot(xy, co)
    width = 2 * ROWS
    down = lax.broadcasted_iota(jnp.int32, (8, width), 0)
    sums, pos = [], jnp.zeros((8, width), F32)
    for g in range(0, NZ, 2):
        u = jnp.concatenate([ref[...] for ref in (u0, u1, u2, u3)[g : g + 2]], axis=0)
        mate = jnp.broadcast_to(jnp.concatenate([here[g : g + 1], here[g + 1 : g + 2]], axis=1), (8, width))
        block = mate >> 7
        total = jnp.zeros((8, width), F32)
        kept = [jnp.zeros((8, width), F32)] * (ROWS // 8)
        for c in range(0, c_ref.shape[0], STRIP):
            s = dot_nt(c_ref[c : c + STRIP], u)
            for k in range(0, STRIP, 8):
                q = k % ROWS // 8
                kept[q] = jnp.where(block == (c + k) // ROWS, s[k : k + 8], kept[q])
            e = expo(s)
            if own_half and g == 0:
                col = lax.broadcasted_iota(jnp.int32, (STRIP, ROWS), 0) + (c - own * ROWS)
                row = lax.broadcasted_iota(jnp.int32, (STRIP, ROWS), 1)
                e = jnp.concatenate([jnp.where(col == row, 0.0, e[:, :ROWS]), e[:, ROWS:]], axis=1)
            for k in range(0, STRIP, 8):
                total = total + e[k : k + 8]
        for q, s in enumerate(kept):
            pos = pos + jnp.where((mate & 127) == down + 8 * q, s, 0.0)
        sums.append(jnp.sum(total, axis=0, keepdims=True))
    sums = jnp.concatenate(sums, axis=1)
    pos = jnp.sum(pos, axis=0, keepdims=True) * INV_TEMP
    rows = [sums[:, r * ROWS : (r + 1) * ROWS] for r in range(NZ)]
    rows.append(pos[:, :ROWS] + pos[:, ROWS:])
    if own_half:
        out_ref = refs[7]
        for q, row in enumerate(rows):
            out_ref[q : q + 1] = row
        out_ref[5:8] = jnp.zeros((3, ROWS), F32)
        return
    in_ref, send_ref = refs[7:]
    rows = [row + in_ref[q : q + 1] for q, row in enumerate(rows)]
    planes = []
    for k in range(NZ):
        r = lax.rem(k - z + NZ, NZ)
        row = rows[0]
        for q in range(1, NZ):
            row = jnp.where(r == q, rows[q], row)
        planes.append(row)
    pos = rows[NZ]
    high = pos.astype(BF16).astype(F32)
    for k in range(NZ):
        q = [planes[(k + r) % NZ] for r in range(NZ)]
        top = jnp.concatenate([q[0], q[1], high], axis=1)
        low = jnp.concatenate([q[2], q[3], pos - high], axis=1)
        piece = jnp.concatenate([top, low], axis=0).astype(BF16)
        for xy_to in range(NXY):
            for co_to in range(NCO):
                send_ref[xy_to * 8 + k * 2 + co_to] = piece


def grads_kernel(blocks, *refs):
    n = len(blocks)
    first = 0 not in blocks
    place_ref, own_ref, other_ref, mate_ref = refs[:4]
    u_refs = refs[4 : 4 + n]
    z, co, xy = place_ref[0], place_ref[1], place_ref[2]
    got_ref = refs[4 + n]
    if first:
        out_refs = refs[5 + n : 5 + 2 * n]
        inv_ref, aux_ref = refs[5 + 2 * n :]
        for k in range(NXY):
            for c in range(NCO):
                got = [got_ref[k * 8 + q * 2 + c, :, 0:ROWS].astype(F32) for q in range(NZ)]
                total = got[0] + got[1] + (got[2] + got[3])
                at = slot(k, c) * ROWS
                inv_ref[c, :, at : at + ROWS] = 1.0 / total[0:1]
        got = [got_ref[xy * 8 + q * 2 + co, :, 0 : 2 * ROWS].astype(F32) for q in range(NZ)]
        total = got[0] + got[1] + (got[2] + got[3])
        for r in range(NZ):
            part = total[r // 2 : r // 2 + 1, r % 2 * ROWS : (r % 2 + 1) * ROWS]
            aux_ref[r : r + 1] = 1.0 / part
        aux_ref[NZ:] = jnp.zeros((8 - NZ, ROWS), F32)
    else:
        inv_ref, aux_ref, *out_refs, loss_ref = refs[5 + n :]
        logs = jnp.zeros((2, 2 * ROWS), F32)
        pos = jnp.zeros((2, ROWS), F32)
        for k in range(NXY):
            for c in range(NCO):
                got = [got_ref[k * 8 + q * 2 + c].astype(F32) for q in range(NZ)]
                got = got[0] + got[1] + (got[2] + got[3])
                pos = pos + got[:, 2 * ROWS :]
                logs = logs + jnp.log(got[:, : 2 * ROWS])
        pos = jnp.sum(pos, axis=0, keepdims=True)
        parts = [logs[r // 2 : r // 2 + 1, r % 2 * ROWS : (r % 2 + 1) * ROWS] for r in range(NZ)]
        loss = -pos
        for k in range(NZ):
            r = lax.rem(k - z + NZ, NZ)
            row = parts[0]
            for q in range(1, NZ):
                row = jnp.where(r == q, parts[q], row)
            loss = loss + row
        loss_ref[...] = jnp.sum(loss, axis=1, keepdims=True) / VIEWS
    own = slot(xy, co)
    inv_row = jnp.concatenate([down_rows(aux_ref[r : r + 1]) for r in blocks], axis=0)
    mates = mate_ref[...]
    u = jnp.concatenate([ref[...] for ref in u_refs], axis=0)
    lane = lax.broadcasted_iota(jnp.int32, (n * ROWS, ROWS), 1)
    total = jnp.zeros((n * ROWS, ROWS), F32)
    for h, c_ref in enumerate((own_ref, other_ref)):
        half = co if h == 0 else 1 - co
        local = local_mates(mates, z, half)
        mate = jnp.concatenate([down_rows(local[r : r + 1]) for r in blocks], axis=0)
        for c in range(0, c_ref.shape[0], CHUNK):
            e = expo(dot_nt(u, c_ref[c : c + CHUNK]))
            if h == 0 and not first:
                col = lax.broadcasted_iota(jnp.int32, e.shape, 1) + (c - own * ROWS)
                row = lax.broadcasted_iota(jnp.int32, e.shape, 0)
                e = jnp.where(col == row, 0.0, e)
            weight = []
            for k in range(0, CHUNK, ROWS):
                w = e[:, k : k + ROWS] * (inv_row + inv_ref[half, :, c + k : c + k + ROWS])
                w = w - jnp.where(mate == lane + (c + k), 2.0, 0.0)
                weight.append(w.astype(BF16))
            total = total + dot_nn(jnp.concatenate(weight, axis=1), c_ref[c : c + CHUNK])
    for q, out_ref in enumerate(out_refs):
        out_ref[...] = total[q * ROWS : (q + 1) * ROWS]


def final_kernel(x_ref, b0, b1, b2, b3, grad_ref):
    x = x_ref[...]
    radius = jnp.sqrt(jnp.sum(x * x, axis=1, keepdims=True) + EPS)
    unit = x / radius
    d = INV_TEMP * (b0[...] + b1[...] + b2[...] + b3[...])
    grad_ref[...] = (d - unit * jnp.sum(unit * d, axis=1, keepdims=True)) / radius


def shift(x, by):
    return lax.ppermute(x, "z", [((k + by) % NZ, k) for k in range(NZ)])


def body(proj, partner):
    y, xh, xl = (lax.axis_index(a) for a in XY)
    z, co = lax.axis_index("z"), lax.axis_index("co")
    xy = (y * 2 + xh) * 2 + xl
    place = jnp.stack([z, co, xy]).astype(jnp.int32)
    unit, copies = call(norm_kernel, [sds((ROWS, ROWS), BF16), sds((NXY, ROWS, ROWS), BF16)])(proj)
    plane = lax.all_to_all(copies, ALL, 0, 0, axis_index_groups=PLANES, tiled=True)
    rows = [unit] + [shift(unit, r) for r in range(1, NZ)]
    mates = partner.reshape(NXY, NZ, NCO, ROWS)
    mates = lax.dynamic_slice(mates, (xy, 0, co, 0), (1, NZ, 1, ROWS)).reshape(NZ, ROWS)
    mates = jnp.concatenate([mates, mates])
    mates = lax.dynamic_slice_in_dim(mates, z, NZ, 0)
    plane, mates, *rows = lax.optimization_barrier((plane, mates, *rows))
    other = lax.ppermute(plane, "co", [(0, 1), (1, 0)])
    cols = NXY * ROWS
    plane = plane.reshape(cols, ROWS)
    other = other.reshape(cols, ROWS)
    n = NZ * ROWS
    work = dict(flops=2 * n * cols * ROWS, nbytes=2**20, exps=n * cols)
    first = call(
        functools.partial(sums_kernel, True), [sds((8, ROWS))], **work
    )(place, *rows, plane, mates)
    (send,) = call(
        functools.partial(sums_kernel, False), [sds((NDEV, 2, 3 * ROWS), BF16)], **work
    )(place, *rows, other, mates, *first)
    got = lax.all_to_all(send, ALL, 0, 0, tiled=True)
    work = dict(flops=6 * n * cols * ROWS, nbytes=2**20, exps=2 * n * cols)
    block = sds((ROWS, ROWS))
    held = (place, plane, other, mates)
    b2, b1, b3, *inv = call(
        functools.partial(grads_kernel, (2, 1, 3)),
        [block] * 3 + [sds((NCO, 1, cols)), sds((8, ROWS))],
        **work,
    )(*held, rows[2], rows[1], rows[3], got)
    b0, loss = call(functools.partial(grads_kernel, (0,)), [block, sds((1, 1))], **work)(*held, rows[0], got, *inv)
    b = {1: b1, 2: b2, 3: b3}
    b = [shift(b[r], -r) for r in (2, 1, 3)] + [b0]
    (grad,) = call(final_kernel, [sds((ROWS, ROWS))])(proj, *b)
    return loss.reshape(()), grad


def solution(mesh):
    fine = Mesh(mesh.devices.reshape(4, 2, 2, 4, 2), ALL)
    return jax.shard_map(
        body,
        mesh=fine,
        in_specs=(P(ALL, None), P()),
        out_specs=(P(), P(ALL, None)),
        check_vma=False,
    )
```

```python
import functools
import math

import jax
import jax.numpy as jnp
from jax import lax
from jax.experimental import pallas as pl
from jax.experimental.pallas import tpu as pltpu
from jax.sharding import Mesh, PartitionSpec as P

EPS = 1e-06
INV_TEMP = 10.0
SCALE = INV_TEMP * math.log2(math.e)

ROWS = 128
NXY = 16
NZ = 4
NCO = 2
NDEV = NXY * NZ * NCO
VIEWS = NDEV * ROWS
XY = ("y", "xh", "xl")
ALL = ("y", "xh", "xl", "z", "co")
FIRST = (13, 5)
PLANES = [
    [(FIRST[c] + k) % NXY * 8 + z * 2 + c for k in range(NXY)] for z in range(NZ) for c in range(NCO)
]
CHUNK = 256
STRIP = 128
F32 = jnp.float32
BF16 = jnp.bfloat16
VMEM = pl.BlockSpec(memory_space=pltpu.VMEM)


def call(body, outs, scratch=(), flops=0, nbytes=0, exps=0):
    def run(*args):
        return pl.pallas_call(
            body,
            out_shape=outs,
            in_specs=[VMEM] * len(args),
            out_specs=[VMEM] * len(outs),
            scratch_shapes=list(scratch),
            compiler_params=pltpu.CompilerParams(vmem_limit_bytes=16 * 2**20),
            cost_estimate=pl.CostEstimate(flops=flops, bytes_accessed=nbytes, transcendentals=exps),
        )(*args)

    return run


def sds(shape, dtype=F32):
    return jax.ShapeDtypeStruct(shape, dtype)


def dot_nt(a, b):
    return lax.dot_general(a, b, (((1,), (1,)), ((), ())), preferred_element_type=F32)


def dot_nn(a, b):
    return lax.dot_general(a, b, (((1,), (0,)), ((), ())), preferred_element_type=F32)


def down_rows(row):
    return jnp.transpose(jnp.broadcast_to(row, (ROWS, ROWS)))


def norm_kernel(x_ref, u_ref, copies_ref):
    x = x_ref[...]
    radius = jnp.sqrt(jnp.sum(x * x, axis=1, keepdims=True) + EPS)
    unit = (x / radius).astype(BF16)
    u_ref[...] = unit
    copies_ref[...] = jnp.broadcast_to(unit[None], (NXY, ROWS, ROWS))


def expo(s):
    return jnp.exp2(s * SCALE)


def position():
    y, xh, xl = (lax.axis_index(a) for a in XY)
    return lax.axis_index("z"), lax.axis_index("co"), (y * 2 + xh) * 2 + xl


def slot(xy, half):
    return (xy - FIRST[0] + (FIRST[0] - FIRST[1]) * half) & (NXY - 1)


def local_mates(mates, z, half):
    here = (((mates >> 8) & 3) == z) & (((mates >> 7) & 1) == half)
    return jnp.where(here, (slot(mates >> 10, half) << 7) | (mates & 127), -1)


def sums_kernel(own_half, *refs):
    u0, u1, u2, u3, c_ref, mate_ref = refs[:6]
    z, co, xy = position()
    half = co if own_half else 1 - co
    mates = mate_ref[...]
    here = local_mates(mates, z, half)
    own = slot(xy, co)
    width = 2 * ROWS
    down = lax.broadcasted_iota(jnp.int32, (8, width), 0)
    sums, pos = [], jnp.zeros((8, width), F32)
    for g in range(0, NZ, 2):
        u = jnp.concatenate([ref[...] for ref in (u0, u1, u2, u3)[g : g + 2]], axis=0)
        mate = jnp.broadcast_to(jnp.concatenate([here[g : g + 1], here[g + 1 : g + 2]], axis=1), (8, width))
        block = mate >> 7
        total = jnp.zeros((8, width), F32)
        kept = [jnp.zeros((8, width), F32)] * (ROWS // 8)
        for c in range(0, c_ref.shape[0], STRIP):
            s = dot_nt(c_ref[c : c + STRIP], u)
            for k in range(0, STRIP, 8):
                q = k % ROWS // 8
                kept[q] = jnp.where(block == (c + k) // ROWS, s[k : k + 8], kept[q])
            e = expo(s)
            if own_half and g == 0:
                col = lax.broadcasted_iota(jnp.int32, (STRIP, ROWS), 0) + (c - own * ROWS)
                row = lax.broadcasted_iota(jnp.int32, (STRIP, ROWS), 1)
                e = jnp.concatenate([jnp.where(col == row, 0.0, e[:, :ROWS]), e[:, ROWS:]], axis=1)
            for k in range(0, STRIP, 8):
                total = total + e[k : k + 8]
        for q, s in enumerate(kept):
            pos = pos + jnp.where((mate & 127) == down + 8 * q, s, 0.0)
        sums.append(jnp.sum(total, axis=0, keepdims=True))
    sums = jnp.concatenate(sums, axis=1)
    pos = jnp.sum(pos, axis=0, keepdims=True) * INV_TEMP
    rows = [sums[:, r * ROWS : (r + 1) * ROWS] for r in range(NZ)]
    rows.append(pos[:, :ROWS] + pos[:, ROWS:])
    if own_half:
        out_ref = refs[6]
        for q, row in enumerate(rows):
            out_ref[q : q + 1] = row
        out_ref[5:8] = jnp.zeros((3, ROWS), F32)
        return
    in_ref, send_ref = refs[6:]
    rows = [row + in_ref[q : q + 1] for q, row in enumerate(rows)]
    planes = []
    for k in range(NZ):
        r = lax.rem(k - z + NZ, NZ)
        row = rows[0]
        for q in range(1, NZ):
            row = jnp.where(r == q, rows[q], row)
        planes.append(row)
    pos = rows[NZ]
    high = pos.astype(BF16).astype(F32)
    for k in range(NZ):
        q = [planes[(k + r) % NZ] for r in range(NZ)]
        top = jnp.concatenate([q[0], q[1], high], axis=1)
        low = jnp.concatenate([q[2], q[3], pos - high], axis=1)
        piece = jnp.concatenate([top, low], axis=0).astype(BF16)
        for xy_to in range(NXY):
            for co_to in range(NCO):
                send_ref[xy_to * 8 + k * 2 + co_to] = piece


def grads_kernel(blocks, *refs):
    n = len(blocks)
    first = 0 not in blocks
    own_ref, other_ref, mate_ref = refs[:3]
    u_refs = refs[3 : 3 + n]
    z, co, xy = position()
    got_ref = refs[3 + n]
    if first:
        out_refs = refs[4 + n : 4 + 2 * n]
        inv_ref, aux_ref = refs[4 + 2 * n :]
        for k in range(NXY):
            for c in range(NCO):
                got = [got_ref[k * 8 + q * 2 + c, :, 0:ROWS].astype(F32) for q in range(NZ)]
                total = got[0] + got[1] + (got[2] + got[3])
                at = slot(k, c) * ROWS
                inv_ref[c, :, at : at + ROWS] = 1.0 / total[0:1]
        got = [got_ref[xy * 8 + q * 2 + co, :, 0 : 2 * ROWS].astype(F32) for q in range(NZ)]
        total = got[0] + got[1] + (got[2] + got[3])
        for r in range(NZ):
            part = total[r // 2 : r // 2 + 1, r % 2 * ROWS : (r % 2 + 1) * ROWS]
            aux_ref[r : r + 1] = 1.0 / part
        aux_ref[NZ:] = jnp.zeros((8 - NZ, ROWS), F32)
    else:
        inv_ref, aux_ref, *out_refs, loss_ref = refs[4 + n :]
        logs = jnp.zeros((2, 2 * ROWS), F32)
        pos = jnp.zeros((2, ROWS), F32)
        for k in range(NXY):
            for c in range(NCO):
                got = [got_ref[k * 8 + q * 2 + c].astype(F32) for q in range(NZ)]
                got = got[0] + got[1] + (got[2] + got[3])
                pos = pos + got[:, 2 * ROWS :]
                logs = logs + jnp.log(got[:, : 2 * ROWS])
        pos = jnp.sum(pos, axis=0, keepdims=True)
        parts = [logs[r // 2 : r // 2 + 1, r % 2 * ROWS : (r % 2 + 1) * ROWS] for r in range(NZ)]
        loss = -pos
        for k in range(NZ):
            r = lax.rem(k - z + NZ, NZ)
            row = parts[0]
            for q in range(1, NZ):
                row = jnp.where(r == q, parts[q], row)
            loss = loss + row
        loss_ref[...] = jnp.sum(loss, axis=1, keepdims=True) / VIEWS
    own = slot(xy, co)
    inv_row = jnp.concatenate([down_rows(aux_ref[r : r + 1]) for r in blocks], axis=0)
    mates = mate_ref[...]
    u = jnp.concatenate([ref[...] for ref in u_refs], axis=0)
    lane = lax.broadcasted_iota(jnp.int32, (n * ROWS, ROWS), 1)
    total = jnp.zeros((n * ROWS, ROWS), F32)
    for h, c_ref in enumerate((own_ref, other_ref)):
        half = co if h == 0 else 1 - co
        local = local_mates(mates, z, half)
        mate = jnp.concatenate([down_rows(local[r : r + 1]) for r in blocks], axis=0)
        for c in range(0, c_ref.shape[0], CHUNK):
            e = expo(dot_nt(u, c_ref[c : c + CHUNK]))
            if h == 0 and not first:
                col = lax.broadcasted_iota(jnp.int32, e.shape, 1) + (c - own * ROWS)
                row = lax.broadcasted_iota(jnp.int32, e.shape, 0)
                e = jnp.where(col == row, 0.0, e)
            weight = []
            for k in range(0, CHUNK, ROWS):
                w = e[:, k : k + ROWS] * (inv_row + inv_ref[half, :, c + k : c + k + ROWS])
                w = w - jnp.where(mate == lane + (c + k), 2.0, 0.0)
                weight.append(w.astype(BF16))
            total = total + dot_nn(jnp.concatenate(weight, axis=1), c_ref[c : c + CHUNK])
    for q, out_ref in enumerate(out_refs):
        out_ref[...] = total[q * ROWS : (q + 1) * ROWS]


def final_kernel(x_ref, b0, b1, b2, b3, grad_ref):
    x = x_ref[...]
    radius = jnp.sqrt(jnp.sum(x * x, axis=1, keepdims=True) + EPS)
    unit = x / radius
    d = INV_TEMP * (b0[...] + b1[...] + b2[...] + b3[...])
    grad_ref[...] = (d - unit * jnp.sum(unit * d, axis=1, keepdims=True)) / radius


def shift(x, by):
    return lax.ppermute(x, "z", [((k + by) % NZ, k) for k in range(NZ)])


def body(proj, partner):
    z, co, xy = position()
    unit, copies = call(norm_kernel, [sds((ROWS, ROWS), BF16), sds((NXY, ROWS, ROWS), BF16)])(proj)
    plane = lax.all_to_all(copies, ALL, 0, 0, axis_index_groups=PLANES, tiled=True)
    rows = [unit] + [shift(unit, r) for r in range(1, NZ)]
    mates = partner.reshape(NXY, NZ, NCO, ROWS)
    mates = lax.dynamic_slice(mates, (xy, 0, co, 0), (1, NZ, 1, ROWS)).reshape(NZ, ROWS)
    mates = jnp.concatenate([mates, mates])
    mates = lax.dynamic_slice_in_dim(mates, z, NZ, 0)
    plane, mates, *rows = lax.optimization_barrier((plane, mates, *rows))
    other = lax.ppermute(plane, "co", [(0, 1), (1, 0)])
    cols = NXY * ROWS
    plane = plane.reshape(cols, ROWS)
    other = other.reshape(cols, ROWS)
    n = NZ * ROWS
    work = dict(flops=2 * n * cols * ROWS, nbytes=2**20, exps=n * cols)
    first = call(
        functools.partial(sums_kernel, True), [sds((8, ROWS))], **work
    )(*rows, plane, mates)
    (send,) = call(
        functools.partial(sums_kernel, False), [sds((NDEV, 2, 3 * ROWS), BF16)], **work
    )(*rows, other, mates, *first)
    got = lax.all_to_all(send, ALL, 0, 0, tiled=True)
    work = dict(flops=6 * n * cols * ROWS, nbytes=2**20, exps=2 * n * cols)
    block = sds((ROWS, ROWS))
    held = (plane, other, mates)
    b2, b1, b3, *inv = call(
        functools.partial(grads_kernel, (2, 1, 3)),
        [block] * 3 + [sds((NCO, 1, cols)), sds((8, ROWS))],
        **work,
    )(*held, rows[2], rows[1], rows[3], got)
    b0, loss = call(functools.partial(grads_kernel, (0,)), [block, sds((1, 1))], **work)(*held, rows[0], got, *inv)
    b = {1: b1, 2: b2, 3: b3}
    b = [shift(b[r], -r) for r in (2, 1, 3)] + [b0]
    (grad,) = call(final_kernel, [sds((ROWS, ROWS))])(proj, *b)
    return loss.reshape(()), grad


def solution(mesh):
    fine = Mesh(mesh.devices.reshape(4, 2, 2, 4, 2), ALL)
    return jax.shard_map(
        body,
        mesh=fine,
        in_specs=(P(ALL, None), P()),
        out_specs=(P(), P(ALL, None)),
        check_vma=False,
    )
```

```python
import functools
import math

import jax
import jax.numpy as jnp
from jax import lax
from jax.experimental import pallas as pl
from jax.experimental.pallas import tpu as pltpu
from jax.sharding import Mesh, PartitionSpec as P

EPS = 1e-06
INV_TEMP = 10.0
SCALE = INV_TEMP * math.log2(math.e)

ROWS = 128
NXY = 16
NZ = 4
NCO = 2
NDEV = NXY * NZ * NCO
VIEWS = NDEV * ROWS
XY = ("y", "xh", "xl")
ALL = ("y", "xh", "xl", "z", "co")
FIRST = (13, 5)
PLANES = [
    [(FIRST[c] + k) % NXY * 8 + z * 2 + c for k in range(NXY)] for z in range(NZ) for c in range(NCO)
]
CHUNK = 256
STRIP = 128
F32 = jnp.float32
BF16 = jnp.bfloat16
VMEM = pl.BlockSpec(memory_space=pltpu.VMEM)


def call(body, outs, scratch=(), flops=0, nbytes=0, exps=0):
    def run(*args):
        return pl.pallas_call(
            body,
            out_shape=outs,
            in_specs=[VMEM] * len(args),
            out_specs=[VMEM] * len(outs),
            scratch_shapes=list(scratch),
            compiler_params=pltpu.CompilerParams(vmem_limit_bytes=16 * 2**20),
            cost_estimate=pl.CostEstimate(flops=flops, bytes_accessed=nbytes, transcendentals=exps),
        )(*args)

    return run


def sds(shape, dtype=F32):
    return jax.ShapeDtypeStruct(shape, dtype)


def dot_nt(a, b):
    return lax.dot_general(a, b, (((1,), (1,)), ((), ())), preferred_element_type=F32)


def dot_nn(a, b):
    return lax.dot_general(a, b, (((1,), (0,)), ((), ())), preferred_element_type=F32)


def down_rows(row):
    return jnp.transpose(jnp.broadcast_to(row, (ROWS, ROWS)))


def norm_kernel(x_ref, u_ref, copies_ref):
    x = x_ref[...]
    radius = jnp.sqrt(jnp.sum(x * x, axis=1, keepdims=True) + EPS)
    unit = (x / radius).astype(BF16)
    u_ref[...] = unit
    copies_ref[...] = jnp.broadcast_to(unit[None], (NXY, ROWS, ROWS))


def expo(s):
    return jnp.exp2(s * SCALE)


def position():
    y, xh, xl = (lax.axis_index(a) for a in XY)
    return lax.axis_index("z"), lax.axis_index("co"), (y * 2 + xh) * 2 + xl


def slot(xy, half):
    return (xy - FIRST[0] + (FIRST[0] - FIRST[1]) * half) & (NXY - 1)


def local_mates(mates, z, half):
    here = (((mates >> 8) & 3) == z) & (((mates >> 7) & 1) == half)
    return jnp.where(here, (slot(mates >> 10, half) << 7) | (mates & 127), -1)


def sums_kernel(own_half, *refs):
    u0, u1, u2, u3, c_ref, mate_ref = refs[:6]
    z, co, xy = position()
    half = co if own_half else 1 - co
    mates = mate_ref[...]
    here = local_mates(mates, z, half)
    own = slot(xy, co)
    width = 2 * ROWS
    down = lax.broadcasted_iota(jnp.int32, (8, width), 0)
    sums, pos = [], jnp.zeros((8, width), F32)
    for g in range(0, NZ, 2):
        u = jnp.concatenate([ref[...] for ref in (u0, u1, u2, u3)[g : g + 2]], axis=0)
        mate = jnp.broadcast_to(jnp.concatenate([here[g : g + 1], here[g + 1 : g + 2]], axis=1), (8, width))
        block = mate >> 7
        total = jnp.zeros((8, width), F32)
        kept = [jnp.zeros((8, width), F32)] * (ROWS // 8)
        for c in range(0, c_ref.shape[0], STRIP):
            s = dot_nt(c_ref[c : c + STRIP], u)
            for k in range(0, STRIP, 8):
                q = k % ROWS // 8
                kept[q] = jnp.where(block == (c + k) // ROWS, s[k : k + 8], kept[q])
            e = expo(s)
            if own_half and g == 0:
                col = lax.broadcasted_iota(jnp.int32, (STRIP, ROWS), 0) + (c - own * ROWS)
                row = lax.broadcasted_iota(jnp.int32, (STRIP, ROWS), 1)
                e = jnp.concatenate([jnp.where(col == row, 0.0, e[:, :ROWS]), e[:, ROWS:]], axis=1)
            for k in range(0, STRIP, 8):
                total = total + e[k : k + 8]
        for q, s in enumerate(kept):
            pos = pos + jnp.where((mate & 127) == down + 8 * q, s, 0.0)
        sums.append(jnp.sum(total, axis=0, keepdims=True))
    sums = jnp.concatenate(sums, axis=1)
    pos = jnp.sum(pos, axis=0, keepdims=True) * INV_TEMP
    rows = [sums[:, r * ROWS : (r + 1) * ROWS] for r in range(NZ)]
    rows.append(pos[:, :ROWS] + pos[:, ROWS:])
    if own_half:
        out_ref = refs[6]
        for q, row in enumerate(rows):
            out_ref[q : q + 1] = row
        out_ref[5:8] = jnp.zeros((3, ROWS), F32)
        return
    in_ref, send_ref = refs[6:]
    rows = [row + in_ref[q : q + 1] for q, row in enumerate(rows)]
    planes = []
    for k in range(NZ):
        r = lax.rem(k - z + NZ, NZ)
        row = rows[0]
        for q in range(1, NZ):
            row = jnp.where(r == q, rows[q], row)
        planes.append(row)
    pos = rows[NZ]
    high = pos.astype(BF16).astype(F32)
    for k in range(NZ):
        q = [planes[(k + r) % NZ] for r in range(NZ)]
        top = jnp.concatenate([q[0], q[1], high], axis=1)
        low = jnp.concatenate([q[2], q[3], pos - high], axis=1)
        piece = jnp.concatenate([top, low], axis=0).astype(BF16)
        for xy_to in range(NXY):
            for co_to in range(NCO):
                send_ref[xy_to * 8 + k * 2 + co_to] = piece


def grads_kernel(blocks, *refs):
    n = len(blocks)
    first = 0 not in blocks
    own_ref, other_ref, mate_ref = refs[:3]
    u_refs = refs[3 : 3 + n]
    z, co, xy = position()
    got_ref = refs[3 + n]
    if first:
        out_refs = refs[4 + n : 4 + 2 * n]
        inv_ref, aux_ref = refs[4 + 2 * n :]
        for k in range(NXY):
            for c in range(NCO):
                got = [got_ref[k * 8 + q * 2 + c, :, 0:ROWS].astype(F32) for q in range(NZ)]
                total = got[0] + got[1] + (got[2] + got[3])
                at = slot(k, c) * ROWS
                inv_ref[c, :, at : at + ROWS] = 1.0 / total[0:1]
        got = [got_ref[xy * 8 + q * 2 + co, :, 0 : 2 * ROWS].astype(F32) for q in range(NZ)]
        total = got[0] + got[1] + (got[2] + got[3])
        for r in range(NZ):
            part = total[r // 2 : r // 2 + 1, r % 2 * ROWS : (r % 2 + 1) * ROWS]
            aux_ref[r : r + 1] = 1.0 / part
        aux_ref[NZ:] = jnp.zeros((8 - NZ, ROWS), F32)
    else:
        inv_ref, aux_ref, *out_refs, loss_ref = refs[4 + n :]
        logs = jnp.zeros((2, 2 * ROWS), F32)
        pos = jnp.zeros((2, ROWS), F32)
        for k in range(NXY):
            for c in range(NCO):
                got = [got_ref[k * 8 + q * 2 + c].astype(F32) for q in range(NZ)]
                got = got[0] + got[1] + (got[2] + got[3])
                pos = pos + got[:, 2 * ROWS :]
                logs = logs + jnp.log(got[:, : 2 * ROWS])
        pos = jnp.sum(pos, axis=0, keepdims=True)
        parts = [logs[r // 2 : r // 2 + 1, r % 2 * ROWS : (r % 2 + 1) * ROWS] for r in range(NZ)]
        loss = -pos
        for k in range(NZ):
            r = lax.rem(k - z + NZ, NZ)
            row = parts[0]
            for q in range(1, NZ):
                row = jnp.where(r == q, parts[q], row)
            loss = loss + row
        loss_ref[...] = jnp.sum(loss, axis=1, keepdims=True) / VIEWS
    own = slot(xy, co)
    inv_row = jnp.concatenate([down_rows(aux_ref[r : r + 1]) for r in blocks], axis=0)
    mates = mate_ref[...]
    u = jnp.concatenate([ref[...] for ref in u_refs], axis=0)
    lane = lax.broadcasted_iota(jnp.int32, (n * ROWS, ROWS), 1)
    total = jnp.zeros((n * ROWS, ROWS), F32)
    for h, c_ref in enumerate((own_ref, other_ref)):
        half = co if h == 0 else 1 - co
        local = local_mates(mates, z, half)
        mate = jnp.concatenate([down_rows(local[r : r + 1]) for r in blocks], axis=0)
        for c in range(0, c_ref.shape[0], CHUNK):
            e = expo(dot_nt(u, c_ref[c : c + CHUNK]))
            if h == 0 and not first:
                col = lax.broadcasted_iota(jnp.int32, e.shape, 1) + (c - own * ROWS)
                row = lax.broadcasted_iota(jnp.int32, e.shape, 0)
                e = jnp.where(col == row, 0.0, e)
            weight = []
            for k in range(0, CHUNK, ROWS):
                w = e[:, k : k + ROWS] * (inv_row + inv_ref[half, :, c + k : c + k + ROWS])
                w = w - jnp.where(mate == lane + (c + k), 2.0, 0.0)
                weight.append(w.astype(BF16))
            total = total + dot_nn(jnp.concatenate(weight, axis=1), c_ref[c : c + CHUNK])
    if not first:
        out_refs[0][...] = total
        return
    u = u.astype(F32)
    along = jnp.sum(u * total, axis=1, keepdims=True)
    for q, out_ref in enumerate(out_refs):
        rows = slice(q * ROWS, (q + 1) * ROWS)
        row = jnp.transpose(jnp.broadcast_to(along[rows], (ROWS, ROWS)))[0:1]
        high = row.astype(BF16).astype(F32)
        out_ref[0:ROWS] = (total[rows] - along[rows] * u[rows]).astype(BF16)
        out_ref[ROWS:] = jnp.concatenate([high, row - high, jnp.zeros((14, ROWS), F32)], axis=0).astype(BF16)


def final_kernel(x_ref, u_ref, b1, b2, b3, b0, grad_ref):
    x = x_ref[...]
    radius = jnp.sqrt(jnp.sum(x * x, axis=1, keepdims=True) + EPS)
    unit = x / radius
    d = b0[...]
    along = jnp.zeros((16, ROWS), F32)
    for b_ref in (b1, b2, b3):
        d = d + b_ref[0:ROWS].astype(F32)
        along = along + b_ref[ROWS:].astype(F32)
    d = d + down_rows(along[0:1] + along[1:2]) * u_ref[...].astype(F32)
    d = INV_TEMP * d
    grad_ref[...] = (d - unit * jnp.sum(unit * d, axis=1, keepdims=True)) / radius


def shift(x, by):
    return lax.ppermute(x, "z", [((k + by) % NZ, k) for k in range(NZ)])


def body(proj, partner):
    z, co, xy = position()
    unit, copies = call(norm_kernel, [sds((ROWS, ROWS), BF16), sds((NXY, ROWS, ROWS), BF16)])(proj)
    plane = lax.all_to_all(copies, ALL, 0, 0, axis_index_groups=PLANES, tiled=True)
    rows = [unit] + [shift(unit, r) for r in range(1, NZ)]
    mates = partner.reshape(NXY, NZ, NCO, ROWS)
    mates = lax.dynamic_slice(mates, (xy, 0, co, 0), (1, NZ, 1, ROWS)).reshape(NZ, ROWS)
    mates = jnp.concatenate([mates, mates])
    mates = lax.dynamic_slice_in_dim(mates, z, NZ, 0)
    plane, mates, *rows = lax.optimization_barrier((plane, mates, *rows))
    other = lax.ppermute(plane, "co", [(0, 1), (1, 0)])
    cols = NXY * ROWS
    plane = plane.reshape(cols, ROWS)
    other = other.reshape(cols, ROWS)
    n = NZ * ROWS
    work = dict(flops=2 * n * cols * ROWS, nbytes=2**20, exps=n * cols)
    first = call(
        functools.partial(sums_kernel, True), [sds((8, ROWS))], **work
    )(*rows, plane, mates)
    (send,) = call(
        functools.partial(sums_kernel, False), [sds((NDEV, 2, 3 * ROWS), BF16)], **work
    )(*rows, other, mates, *first)
    got = lax.all_to_all(send, ALL, 0, 0, tiled=True)
    work = dict(flops=6 * n * cols * ROWS, nbytes=2**20, exps=2 * n * cols)
    block = sds((ROWS, ROWS))
    held = (plane, other, mates)
    b2, b1, b3, *inv = call(
        functools.partial(grads_kernel, (2, 1, 3)),
        [sds((ROWS + 16, ROWS), BF16)] * 3 + [sds((NCO, 1, cols)), sds((8, ROWS))],
        **work,
    )(*held, rows[2], rows[1], rows[3], got)
    b0, loss = call(functools.partial(grads_kernel, (0,)), [block, sds((1, 1))], **work)(*held, rows[0], got, *inv)
    b = {1: b1, 2: b2, 3: b3}
    b = [shift(b[r], -r) for r in (2, 1, 3)] + [b0]
    (grad,) = call(final_kernel, [sds((ROWS, ROWS))])(proj, unit, *b)
    return loss.reshape(()), grad


def solution(mesh):
    fine = Mesh(mesh.devices.reshape(4, 2, 2, 4, 2), ALL)
    return jax.shard_map(
        body,
        mesh=fine,
        in_specs=(P(ALL, None), P()),
        out_specs=(P(), P(ALL, None)),
        check_vma=False,
    )
```

```python
import functools
import math

import jax
import jax.numpy as jnp
from jax import lax
from jax.experimental import pallas as pl
from jax.experimental.pallas import tpu as pltpu
from jax.sharding import Mesh, PartitionSpec as P

EPS = 1e-06
INV_TEMP = 10.0
SCALE = INV_TEMP * math.log2(math.e)

ROWS = 128
NXY = 16
NZ = 4
NCO = 2
NDEV = NXY * NZ * NCO
VIEWS = NDEV * ROWS
XY = ("y", "xh", "xl")
ALL = ("y", "xh", "xl", "z", "co")
FIRST = (13, 5)
PLANES = [
    [(FIRST[c] + k) % NXY * 8 + z * 2 + c for k in range(NXY)] for z in range(NZ) for c in range(NCO)
]
CHUNK = 256
STRIP = 128
F32 = jnp.float32
BF16 = jnp.bfloat16
VMEM = pl.BlockSpec(memory_space=pltpu.VMEM)


def call(body, outs, scratch=(), flops=0, nbytes=0, exps=0):
    def run(*args):
        return pl.pallas_call(
            body,
            out_shape=outs,
            in_specs=[VMEM] * len(args),
            out_specs=[VMEM] * len(outs),
            scratch_shapes=list(scratch),
            compiler_params=pltpu.CompilerParams(vmem_limit_bytes=16 * 2**20),
            cost_estimate=pl.CostEstimate(flops=flops, bytes_accessed=nbytes, transcendentals=exps),
        )(*args)

    return run


def sds(shape, dtype=F32):
    return jax.ShapeDtypeStruct(shape, dtype)


def dot_nt(a, b):
    return lax.dot_general(a, b, (((1,), (1,)), ((), ())), preferred_element_type=F32)


def dot_nn(a, b):
    return lax.dot_general(a, b, (((1,), (0,)), ((), ())), preferred_element_type=F32)


def down_rows(row):
    return jnp.transpose(jnp.broadcast_to(row, (ROWS, ROWS)))


def norm_kernel(x_ref, u_ref, copies_ref):
    x = x_ref[...]
    radius = jnp.sqrt(jnp.sum(x * x, axis=1, keepdims=True) + EPS)
    unit = (x / radius).astype(BF16)
    u_ref[...] = unit
    copies_ref[...] = jnp.broadcast_to(unit[None], (NXY, ROWS, ROWS))


def expo(s):
    return jnp.exp2(s * SCALE)


def position():
    y, xh, xl = (lax.axis_index(a) for a in XY)
    return lax.axis_index("z"), lax.axis_index("co"), (y * 2 + xh) * 2 + xl


def slot(xy, half):
    return (xy - FIRST[0] + (FIRST[0] - FIRST[1]) * half) & (NXY - 1)


def local_mates(mates, z, half):
    here = (((mates >> 8) & 3) == z) & (((mates >> 7) & 1) == half)
    return jnp.where(here, (slot(mates >> 10, half) << 7) | (mates & 127), -1)


def sums_kernel(own_half, *refs):
    u0, u1, u2, u3, c_ref, mate_ref = refs[:6]
    z, co, xy = position()
    half = co if own_half else 1 - co
    mates = mate_ref[...]
    here = local_mates(mates, z, half)
    own = slot(xy, co)
    width = 2 * ROWS
    down = lax.broadcasted_iota(jnp.int32, (8, width), 0)
    sums, pos = [], jnp.zeros((8, width), F32)
    for g in range(0, NZ, 2):
        u = jnp.concatenate([ref[...] for ref in (u0, u1, u2, u3)[g : g + 2]], axis=0)
        mate = jnp.broadcast_to(jnp.concatenate([here[g : g + 1], here[g + 1 : g + 2]], axis=1), (8, width))
        block = mate >> 7
        total = jnp.zeros((8, width), F32)
        kept = [jnp.zeros((8, width), F32)] * (ROWS // 8)
        for c in range(0, c_ref.shape[0], STRIP):
            s = dot_nt(c_ref[c : c + STRIP], u)
            for k in range(0, STRIP, 8):
                q = k % ROWS // 8
                kept[q] = jnp.where(block == (c + k) // ROWS, s[k : k + 8], kept[q])
            e = expo(s)
            if own_half and g == 0:
                col = lax.broadcasted_iota(jnp.int32, (STRIP, ROWS), 0) + (c - own * ROWS)
                row = lax.broadcasted_iota(jnp.int32, (STRIP, ROWS), 1)
                e = jnp.concatenate([jnp.where(col == row, 0.0, e[:, :ROWS]), e[:, ROWS:]], axis=1)
            for k in range(0, STRIP, 8):
                total = total + e[k : k + 8]
        for q, s in enumerate(kept):
            pos = pos + jnp.where((mate & 127) == down + 8 * q, s, 0.0)
        sums.append(jnp.sum(total, axis=0, keepdims=True))
    sums = jnp.concatenate(sums, axis=1)
    pos = jnp.sum(pos, axis=0, keepdims=True) * INV_TEMP
    rows = [sums[:, r * ROWS : (r + 1) * ROWS] for r in range(NZ)]
    rows.append(pos[:, :ROWS] + pos[:, ROWS:])
    if own_half:
        out_ref = refs[6]
        for q, row in enumerate(rows):
            out_ref[q : q + 1] = row
        out_ref[5:8] = jnp.zeros((3, ROWS), F32)
        return
    in_ref, send_ref = refs[6:]
    rows = [row + in_ref[q : q + 1] for q, row in enumerate(rows)]
    planes = []
    for k in range(NZ):
        r = lax.rem(k - z + NZ, NZ)
        row = rows[0]
        for q in range(1, NZ):
            row = jnp.where(r == q, rows[q], row)
        planes.append(row)
    pos = rows[NZ]
    high = pos.astype(BF16).astype(F32)
    for k in range(NZ):
        q = [planes[(k + r) % NZ] for r in range(NZ)]
        top = jnp.concatenate([q[0], q[1], high], axis=1)
        low = jnp.concatenate([q[2], q[3], pos - high], axis=1)
        piece = jnp.concatenate([top, low], axis=0).astype(BF16)
        for xy_to in range(NXY):
            for co_to in range(NCO):
                send_ref[xy_to * 8 + k * 2 + co_to] = piece


def grads_kernel(blocks, *refs):
    n = len(blocks)
    first = 0 not in blocks
    own_ref, other_ref, mate_ref = refs[:3]
    u_refs = refs[3 : 3 + n]
    z, co, xy = position()
    got_ref = refs[3 + n]
    if first:
        out_refs = refs[4 + n : 4 + 2 * n]
        inv_ref, aux_ref = refs[4 + 2 * n :]
        logs = jnp.zeros((2, ROWS), F32)
        for k in range(NXY):
            for c in range(NCO):
                got = [got_ref[k * 8 + q * 2 + c, :, 0:ROWS].astype(F32) for q in range(NZ)]
                total = got[0] + got[1] + (got[2] + got[3])
                logs = logs + jnp.log(total)
                at = slot(k, c) * ROWS
                inv_ref[c, :, at : at + ROWS] = 1.0 / total[0:1]
        got = [got_ref[xy * 8 + q * 2 + co, :, 0 : 2 * ROWS].astype(F32) for q in range(NZ)]
        total = got[0] + got[1] + (got[2] + got[3])
        for r in range(NZ):
            part = total[r // 2 : r // 2 + 1, r % 2 * ROWS : (r % 2 + 1) * ROWS]
            aux_ref[r : r + 1] = 1.0 / part
        logs_high = logs[0:1].astype(BF16).astype(F32)
        logs_low = (logs[0:1] - logs_high).astype(BF16).astype(F32)
        aux_ref[NZ : NZ + 1] = logs_high
        aux_ref[NZ + 1 : NZ + 2] = logs_low
        aux_ref[NZ + 2 :] = jnp.zeros((6 - NZ, ROWS), F32)
    else:
        inv_ref, aux_ref, *out_refs, pos_ref = refs[4 + n :]
        pos = jnp.zeros((2, ROWS), F32)
        for k in range(NDEV):
            pos = pos + got_ref[k, :, 2 * ROWS :].astype(F32)
        pos_ref[...] = jnp.sum(pos, axis=0, keepdims=True)
    own = slot(xy, co)
    inv_row = jnp.concatenate([down_rows(aux_ref[r : r + 1]) for r in blocks], axis=0)
    mates = mate_ref[...]
    u = jnp.concatenate([ref[...] for ref in u_refs], axis=0)
    lane = lax.broadcasted_iota(jnp.int32, (n * ROWS, ROWS), 1)
    total = jnp.zeros((n * ROWS, ROWS), F32)
    for h, c_ref in enumerate((own_ref, other_ref)):
        half = co if h == 0 else 1 - co
        local = local_mates(mates, z, half)
        mate = jnp.concatenate([down_rows(local[r : r + 1]) for r in blocks], axis=0)
        for c in range(0, c_ref.shape[0], CHUNK):
            e = expo(dot_nt(u, c_ref[c : c + CHUNK]))
            if h == 0 and not first:
                col = lax.broadcasted_iota(jnp.int32, e.shape, 1) + (c - own * ROWS)
                row = lax.broadcasted_iota(jnp.int32, e.shape, 0)
                e = jnp.where(col == row, 0.0, e)
            weight = []
            for k in range(0, CHUNK, ROWS):
                w = e[:, k : k + ROWS] * (inv_row + inv_ref[half, :, c + k : c + k + ROWS])
                w = w - jnp.where(mate == lane + (c + k), 2.0, 0.0)
                weight.append(w.astype(BF16))
            total = total + dot_nn(jnp.concatenate(weight, axis=1), c_ref[c : c + CHUNK])
    if not first:
        out_refs[0][...] = total
        return
    u = u.astype(F32)
    along = jnp.sum(u * total, axis=1, keepdims=True)
    for q, out_ref in enumerate(out_refs):
        rows = slice(q * ROWS, (q + 1) * ROWS)
        row = jnp.transpose(jnp.broadcast_to(along[rows], (ROWS, ROWS)))[0:1]
        high = row.astype(BF16).astype(F32)
        out_ref[0:ROWS] = (total[rows] - along[rows] * u[rows]).astype(BF16)
        out_ref[ROWS:] = jnp.concatenate(
            [high, row - high, logs_high, logs_low, jnp.zeros((12, ROWS), F32)], axis=0
        ).astype(BF16)


def final_kernel(x_ref, u_ref, aux_ref, pos_ref, b2, b1, b3, b0, loss_ref, grad_ref):
    z = position()[0]
    x = x_ref[...]
    radius = jnp.sqrt(jnp.sum(x * x, axis=1, keepdims=True) + EPS)
    unit = x / radius
    d = b0[...]
    along = jnp.zeros((1, ROWS), F32)
    logs = [aux_ref[NZ : NZ + 1] + aux_ref[NZ + 1 : NZ + 2]]
    for b_ref in (b1, b2, b3):
        d = d + b_ref[0:ROWS].astype(F32)
        tail = b_ref[ROWS:].astype(F32)
        along = along + (tail[0:1] + tail[1:2])
        logs.append(tail[2:3] + tail[3:4])
    d = d + down_rows(along) * u_ref[...].astype(F32)
    d = INV_TEMP * d
    grad_ref[...] = (d - unit * jnp.sum(unit * d, axis=1, keepdims=True)) / radius
    loss = -pos_ref[...]
    for k in range(NZ):
        r = lax.rem(z - k + NZ, NZ)
        row = logs[0]
        for q in range(1, NZ):
            row = jnp.where(r == q, logs[q], row)
        loss = loss + row
    loss_ref[...] = jnp.sum(loss, axis=1, keepdims=True) / VIEWS


def shift(x, by):
    return lax.ppermute(x, "z", [((k + by) % NZ, k) for k in range(NZ)])


def body(proj, partner):
    z, co, xy = position()
    unit, copies = call(norm_kernel, [sds((ROWS, ROWS), BF16), sds((NXY, ROWS, ROWS), BF16)])(proj)
    plane = lax.all_to_all(copies, ALL, 0, 0, axis_index_groups=PLANES, tiled=True)
    rows = [unit] + [shift(unit, r) for r in range(1, NZ)]
    mates = partner.reshape(NXY, NZ, NCO, ROWS)
    mates = lax.dynamic_slice(mates, (xy, 0, co, 0), (1, NZ, 1, ROWS)).reshape(NZ, ROWS)
    mates = jnp.concatenate([mates, mates])
    mates = lax.dynamic_slice_in_dim(mates, z, NZ, 0)
    plane, mates, *rows = lax.optimization_barrier((plane, mates, *rows))
    other = lax.ppermute(plane, "co", [(0, 1), (1, 0)])
    cols = NXY * ROWS
    plane = plane.reshape(cols, ROWS)
    other = other.reshape(cols, ROWS)
    n = NZ * ROWS
    work = dict(flops=2 * n * cols * ROWS, nbytes=2**20, exps=n * cols)
    first = call(
        functools.partial(sums_kernel, True), [sds((8, ROWS))], **work
    )(*rows, plane, mates)
    (send,) = call(
        functools.partial(sums_kernel, False), [sds((NDEV, 2, 3 * ROWS), BF16)], **work
    )(*rows, other, mates, *first)
    got = lax.all_to_all(send, ALL, 0, 0, tiled=True)
    work = dict(flops=6 * n * cols * ROWS, nbytes=2**20, exps=2 * n * cols)
    block = sds((ROWS, ROWS))
    held = (plane, other, mates)
    b2, b1, b3, *inv = call(
        functools.partial(grads_kernel, (2, 1, 3)),
        [sds((ROWS + 16, ROWS), BF16)] * 3 + [sds((NCO, 1, cols)), sds((8, ROWS))],
        **work,
    )(*held, rows[2], rows[1], rows[3], got)
    b0, pos = call(functools.partial(grads_kernel, (0,)), [block, sds((1, ROWS))], **work)(*held, rows[0], got, *inv)
    b = {1: b1, 2: b2, 3: b3}
    b = [shift(b[r], -r) for r in (2, 1, 3)] + [b0]
    loss, grad = call(final_kernel, [sds((1, 1)), sds((ROWS, ROWS))])(proj, unit, inv[1], pos, *b)
    return loss.reshape(()), grad


def solution(mesh):
    fine = Mesh(mesh.devices.reshape(4, 2, 2, 4, 2), ALL)
    return jax.shard_map(
        body,
        mesh=fine,
        in_specs=(P(ALL, None), P()),
        out_specs=(P(), P(ALL, None)),
        check_vma=False,
    )
```
